512 devices in a mesh: space: 64 (over y, z_hi, x), vec: 8 (over z_lo, core).
Axes of the slice: x: 4, y: 8, z: 8 (z_hi: 2, z_lo: 4; z = z_hi * 4 + z_lo), core: 2. Of those that a mesh axis runs over, the one named last changes fastest.
Arguments:
- node_feat: bfloat16 [8192, 256], P('space'), may hold values from -6 to 6
- radial: bfloat16 [131072, 128], P(('space', 'vec')), may hold values from -6 to 6
- edge_src: int32 [131072], P(('space', 'vec')), may hold values from 0 to 127
- edge_dst: int32 [131072], P(('space', 'vec')), may hold values from 0 to 255
- edge_live: int32 [131072], P(('space', 'vec')), may hold values 0 or 1
- w_src: bfloat16 [256, 256], replicated, may hold values from -0.375 to 0.375
- w_dst: bfloat16 [256, 256], replicated, may hold values from -0.375 to 0.375
- w_radial: bfloat16 [128, 256], replicated, may hold values from -0.5 to 0.5
- w_hidden: bfloat16 [2, 256, 256], replicated, may hold values from -0.375 to 0.375
- w_out: bfloat16 [169, 256], replicated, may hold values from -0.01953125 to 0.01953125
- start_vectors: float32 [32, 13, 8192], P('vec', None, 'space'), may hold values from -6 to 6
Outputs:
- pair_blocks: bfloat16 [169, 131072], P(None, ('space', 'vec'))
- filtered: float32 [32, 13, 8192], P('vec', None, 'space')
The draws below stay inside these ranges and needn't reach their ends.
Inputs may be any that keep to these rules, and one draw needn't show every extreme that they name: `edge_dst`: A value below 128 names an atom of the slot's own domain; a value k of 128 or more names atom k - 128 of the next domain, the first domain following the last.
All inputs are finite; a program needn't handle non-finite values. No bound on the sum of `edge_live` on one device may be relied on, other than what follows from the above.
Results may differ from the reference program's by a relative error of at most 0.0062.
Values may be sent and summed in bfloat16 or wider, within the bound.
A program may use at most 64 MiB of HBM per device.

```python
import jax
import jax.numpy as jnp
from jax import lax

W = 256
ORB = 13
R = 128
LAYERS = 2
NV = 32
ATOM_DEV = 128
ATOMS = 8192
EDGE_DOM = 2048
EDGES = 131072
N_SPACE = 64


def plant(entries, stream_key, least, largest):
    dims = entries.shape
    place = [jax.random.randint(jax.random.fold_in(stream_key, axis), (), 0, dims[axis]) for axis in range(len(dims))]
    entries = entries.at[tuple(place)].set(least)
    longest = dims.index(max(dims))
    place[longest] = (place[longest] + 1) % dims[longest]
    return entries.at[tuple(place)].set(largest)


def steps_of(rng, extent, cuts, least, top_value):
    loudness = 1.0
    for axis_at, shards_of in cuts:
        draws = jax.random.uniform(jax.random.fold_in(jax.random.fold_in(rng, 6), axis_at), (shards_of,), jnp.float32, least / len(cuts), top_value / len(cuts))
        loudness = loudness * jnp.repeat(jnp.exp(draws), extent[axis_at] // shards_of).reshape((-1,) + (1,) * (len(extent) - 1 - axis_at))
    return loudness


def normal_values(stream_key, extent, scale, limit, shards=(), held_as=jnp.bfloat16):
    gain = steps_of(stream_key, extent, shards, -0.22, 0.18) if shards else 1.0
    array = jax.random.normal(stream_key, extent, jnp.float32) * scale * gain
    return jnp.minimum(jnp.maximum(array, -limit), limit).astype(held_as)


def setup_inputs(seed: int = 0) -> dict:
    seeds = jax.random.split(jax.random.key(seed), 12)
    return {
        "node_feat": normal_values(seeds[0], (ATOMS, W), 1.0, 6.0, ((0, 64),)),
        "radial": normal_values(seeds[1], (EDGES, R), 1.0, 6.0, ((0, 512),)),
        "edge_src": plant(jax.random.randint(seeds[2], (EDGES,), 0, ATOM_DEV), jax.random.fold_in(seeds[2], 1), 0, ATOM_DEV - 1).astype(jnp.int32),
        "edge_dst": plant(jax.random.randint(seeds[3], (EDGES,), 0, 2 * ATOM_DEV), jax.random.fold_in(seeds[3], 1), 0, (2 * ATOM_DEV) - 1).astype(jnp.int32),
        "edge_live": plant((jax.random.randint(seeds[4], (EDGES,), 0, 4) < 3).astype(jnp.int32), jax.random.fold_in(seeds[4], 1), 0, 1),
        "w_src": normal_values(seeds[5], (W, W), W ** -0.5, 0.375),
        "w_dst": normal_values(seeds[6], (W, W), W ** -0.5, 0.375),
        "w_radial": normal_values(seeds[7], (R, W), R ** -0.5, 0.5),
        "w_hidden": normal_values(seeds[8], (LAYERS, W, W), W ** -0.5, 0.375),
        "w_out": normal_values(seeds[9], (ORB * ORB, W), (W * ORB * 2 * EDGE_DOM // ATOM_DEV) ** -0.5, 0.01953125),
        "start_vectors": normal_values(seeds[10], (NV, ORB, ATOMS), 1.0, 6.0, ((0, 8), (2, 64)), jnp.float32),
    }


def apply_pairs(blocks, sources, targets, vectors):
    at_targets = jnp.take(vectors, targets, axis=2)
    at_sources = jnp.take(vectors, sources, axis=2)
    to_first = jnp.einsum("abe,vbe->vae", blocks, at_targets, precision=lax.Precision.HIGHEST)
    to_second = jnp.einsum("bae,vbe->vae", blocks, at_sources, precision=lax.Precision.HIGHEST)
    result = jnp.zeros(vectors.shape, jnp.float32)
    result = result.at[:, :, sources].add(to_first)
    return result.at[:, :, targets].add(to_second)


def edge_layer(feat_own, feat_next, radial, sources, targets, live, w_src, w_dst, w_radial, w_hidden, w_out):
    extended = jnp.concatenate([feat_own, feat_next], 0)
    proj_src = jnp.dot(feat_own, w_src, preferred_element_type=jnp.float32)
    proj_dst = jnp.dot(extended, w_dst, preferred_element_type=jnp.float32)
    pre = proj_src[sources] + proj_dst[targets] + jnp.dot(radial, w_radial, preferred_element_type=jnp.float32)
    hidden = jax.nn.silu(pre).astype(jnp.bfloat16)
    for layer in range(LAYERS):
        update = jax.nn.silu(jnp.dot(hidden, w_hidden[layer], preferred_element_type=jnp.float32))
        hidden = (hidden.astype(jnp.float32) + update).astype(jnp.bfloat16)
    raw = lax.dot_general(w_out, hidden, (((1,), (1,)), ((), ())), preferred_element_type=jnp.float32)
    return (raw * live.astype(jnp.float32)[None, :]).astype(jnp.bfloat16)


def reference(node_feat, radial, edge_src, edge_dst, edge_live, w_src, w_dst, w_radial, w_hidden, w_out, start_vectors):
    feats = node_feat.reshape(N_SPACE, ATOM_DEV, W)
    feats_next = jnp.roll(feats, -1, axis=0)
    radial_dom = radial.reshape(N_SPACE, EDGE_DOM, R)
    src_dom = edge_src.reshape(N_SPACE, EDGE_DOM)
    dst_dom = edge_dst.reshape(N_SPACE, EDGE_DOM)
    live_dom = edge_live.reshape(N_SPACE, EDGE_DOM)

    def one_domain(items):
        return edge_layer(items[0], items[1], items[2], items[3], items[4], items[5], w_src, w_dst, w_radial, w_hidden, w_out)

    blocks_dom = lax.map(one_domain, (feats, feats_next, radial_dom, src_dom, dst_dom, live_dom))
    pair_blocks = jnp.transpose(blocks_dom, (1, 0, 2)).reshape(ORB * ORB, EDGES)

    def operator(vectors):
        moved = jnp.moveaxis(vectors.reshape(NV, ORB, N_SPACE, ATOM_DEV), 2, 0)
        extended = jnp.concatenate([moved, jnp.roll(moved, -1, axis=0)], axis=3)

        def one_apply(items):
            blocks = items[0].astype(jnp.float32).reshape(ORB, ORB, EDGE_DOM)
            return apply_pairs(blocks, items[1], items[2], items[3])

        result_ext = lax.map(one_apply, (blocks_dom, src_dom, dst_dom, extended))
        result = result_ext[..., :ATOM_DEV] + jnp.roll(result_ext[..., ATOM_DEV:], 1, axis=0)
        return jnp.moveaxis(result, 0, 2).reshape(NV, ORB, ATOMS)

    first = operator(start_vectors)
    filtered = 2.0 * operator(first) - start_vectors
    return pair_blocks, filtered
```

```python
import math

import jax
import jax.numpy as jnp
from jax import lax
from jax.experimental import pallas as pl
from jax.experimental.pallas import tpu as pltpu
from jax.sharding import PartitionSpec as P

F32, BF16 = jnp.float32, jnp.bfloat16
MESH = pl.DeviceIdType.MESH
CHIPS = 4
SLOTS = [(k, r) for k in range(CHIPS) for r in range(2)]
PEERS = SLOTS[1:]
PAD = 16


def silu(v):
    half = 0.5 * v
    return half + half * jnp.tanh(half)


def mm(a, b):
    return jnp.dot(a, b, preferred_element_type=F32)


def mm_nt(a, b):
    return lax.dot_general(a, b, (((1,), (1,)), ((), ())), preferred_element_type=F32)


def transposed(x):
    return x.astype(F32).T.astype(BF16)


def kernel(
    feat_hbm, radial_hbm, src_ref, dst_ref, live_ref, ws_hbm, wd_hbm, wr_hbm, wh_hbm, wo_hbm, sv_hbm,
    blocks_hbm, out_ref,
    feat, ghost, rad, ws, wd, wr, wh, wo, sv,
    info, onehot, ha, hb, xs, xt, ys, yt,
    v_own, v_gh, proj, wht, wrt, wa, pb, blocks,
    gh_out, own_out, gh_in, own_in, gh2_out, gh2_in,
    local_sem, send_sem, recv_sem,
):
    n_space = lax.axis_size("space")
    d = lax.axis_index("space")
    j = lax.axis_index("vec")
    z, c = j // 2, j % 2
    zk = [z, z + 1 - 2 * (z % 2), (z + 2) % 4, 3 - z]
    left = (lax.rem(d + n_space - 1, n_space), j)
    right = (lax.rem(d + 1, n_space), j)
    at = [[(d, zk[k] * 2 + (c if r == 0 else 1 - c)) for r in range(2)] for k in range(CHIPS)]
    orb = out_ref.shape[1]
    nv = out_ref.shape[0]

    barrier = pltpu.get_barrier_semaphore()
    for dev in [left, right] + [at[k][r] for k, r in PEERS]:
        pl.semaphore_signal(barrier, inc=1, device_id=dev, device_id_type=MESH)

    loads = []
    for i, (a, b) in enumerate(
        [(sv_hbm, sv), (feat_hbm, feat), (ws_hbm, ws), (wd_hbm, wd), (wr_hbm, wr), (wh_hbm, wh), (wo_hbm, wo), (radial_hbm, rad.at[0])]
    ):
        cp = pltpu.make_async_copy(a, b, local_sem.at[i])
        cp.start()
        loads.append(cp)

    for row, ref in enumerate((src_ref, dst_ref, live_ref)):
        for h in range(2):
            info[0, 2 * row + h : 2 * row + h + 1, :] = ref[h * 128 : (h + 1) * 128].reshape(1, 128)
    info[0, 6:8, :] = jnp.zeros((2, 128), jnp.int32)
    loads[0].wait()
    v_own[...] = jnp.zeros_like(v_own)
    start = jnp.concatenate(
        [jnp.concatenate([sv[v], jnp.zeros((PAD - orb, 128), F32)], 0) for v in range(nv)], 0
    )
    v_own[0] = start.astype(BF16)

    pl.semaphore_wait(barrier, 2 + len(PEERS))

    sent = []

    def send(i, a, b, dev):
        cp = pltpu.make_async_remote_copy(
            src_ref=a, dst_ref=b, send_sem=send_sem.at[i], recv_sem=recv_sem.at[i],
            device_id=dev, device_id_type=MESH,
        )
        cp.start()
        sent.append(cp)
        return cp

    mine = pl.ds(pl.multiple_of(j * 16, 16), 16)
    piece_in = send(0, feat_hbm.at[mine, :], ghost.at[mine, :], left)
    info_in = {}
    for n, (k, r) in enumerate(PEERS):
        s = 2 * k + r
        info_in[s] = send(5 + n, info.at[0], info.at[s], at[k][r])
    rad_in = {}
    for k in (1, 3, 2):
        rad_in[k] = send(1 + k, radial_hbm, rad.at[k], at[k][0])
    vgh_in = send(1, v_own.at[0], v_gh.at[0], left)

    def make_onehot(s):
        rows = lax.broadcasted_iota(jnp.int32, (256, 128), 0)
        for h in range(2):
            lanes = slice(h * 128, (h + 1) * 128)
            onehot[s, 0:128, lanes] = jnp.where(rows[:128] == info[s, h : h + 1, :], 1.0, 0.0).astype(BF16)
            onehot[s, 128:384, lanes] = jnp.where(rows == info[s, 2 + h : 3 + h, :], 1.0, 0.0).astype(BF16)

    make_onehot(0)
    for cp in loads[1:]:
        cp.wait()

    piece_in.wait_recv()
    ghost_in = []
    for n, (k, r) in enumerate(PEERS):
        ghost_in.append(send(12 + n, ghost.at[mine, :], ghost.at[mine, :], at[k][r]))

    for layer in range(wh.shape[0]):
        wht[layer] = transposed(wh[layer])
    wrt[...] = transposed(wr[...])
    rows = lax.broadcasted_iota(jnp.int32, (13 * PAD, 169), 0)
    cols = lax.broadcasted_iota(jnp.int32, (13 * PAD, 169), 1)
    outer, inner = lax.shift_right_logical(rows, 4), lax.bitwise_and(rows, 15)
    spread = jnp.where((inner < orb) & (cols == outer * orb + inner), 1.0, 0.0).astype(BF16)
    wa[...] = mm(spread, wo[...]).astype(BF16)
    rows = lax.broadcasted_iota(jnp.int32, (13 * PAD, 13 * PAD), 0)
    cols = lax.broadcasted_iota(jnp.int32, (13 * PAD, 13 * PAD), 1)
    outer, inner = lax.shift_right_logical(rows, 4), lax.bitwise_and(rows, 15)
    pb[...] = jnp.where((inner < orb) & (cols == inner * PAD + outer), 1.0, 0.0).astype(BF16)
    proj[:, 0:128] = transposed(mm(feat[...], ws[...]))
    proj[:, 128:256] = transposed(mm(feat[...], wd[...]))

    for k, r in PEERS:
        s = 2 * k + r
        info_in[s].wait_recv()
        make_onehot(s)

    for cp in ghost_in:
        cp.wait_recv()
    proj[:, 256:384] = transposed(mm(ghost[...], wd[...]))

    def live_row(s):
        return jnp.concatenate([info[s, 4:5, :], info[s, 5:6, :]], 1).astype(F32)

    def network(k):
        s = 2 * k
        pre = mm(proj[...], onehot[s]) + mm_nt(wrt[...], rad[k])
        hidden = silu(pre).astype(BF16)
        for layer in range(wh.shape[0]):
            hidden = (hidden.astype(F32) + silu(mm(wht[layer], hidden))).astype(BF16)
        live = live_row(s)
        ha[s] = (mm(wa[...], hidden) * live).astype(BF16)
        if k == 0:
            blocks[...] = (mm(wo[...], hidden) * live).astype(BF16)

    def to_targets(s, vec):
        xs[...] = mm(vec, onehot[s, 0:128, :]).reshape(nv, PAD, 256)
        acc = jnp.zeros((nv, PAD, 256), F32)
        for a in range(orb):
            acc += ha[s, a * PAD : (a + 1) * PAD, :].astype(F32)[None] * xs[:, a : a + 1, :]
        return acc.reshape(nv * PAD, 256).astype(BF16)

    def to_sources(s, vec):
        xt[...] = mm(vec, onehot[s, 128:384, :]).reshape(nv, PAD, 256)
        acc = jnp.zeros((nv, PAD, 256), F32)
        for b in range(orb):
            acc += hb[s, b * PAD : (b + 1) * PAD, :][None] * xt[:, b : b + 1, :]
        return acc.reshape(nv * PAD, 256).astype(BF16)

    def at_targets(s, y):
        return mm_nt(y, onehot[s, 128:384, :])

    def at_sources(s, y):
        return mm_nt(y, onehot[s, 0:128, :])

    h_in = []
    p_t = jnp.zeros((nv * PAD, 256), F32)
    p_s = jnp.zeros((nv * PAD, 128), F32)

    def first_apply(s):
        hb[s] = mm(pb[...], ha[s])
        own = v_own[0]
        both = jnp.concatenate([own, v_gh[0]], 1)
        return at_targets(s, to_targets(s, own)), at_sources(s, to_sources(s, both))

    for k in range(CHIPS):
        if k:
            rad_in[k].wait_recv()
        network(k)
        h_in.append(send(19 + k, ha.at[2 * k], ha.at[2 * k + 1], at[0][1]))
        if k == 0:
            blocks_out = pltpu.make_async_copy(blocks, blocks_hbm, local_sem.at[8])
            blocks_out.start()
            vgh_in.wait_recv()
        dt, ds = first_apply(2 * k)
        p_t, p_s = p_t + dt, p_s + ds
        h_in[k].wait_recv()
        dt, ds = first_apply(2 * k + 1)
        p_t, p_s = p_t + dt, p_s + ds

    part_gh = p_t[:, 128:]
    part_own = p_s + p_t[:, :128]
    gh_out[...] = part_gh.astype(BF16)
    gh_in_cp = send(23, gh_out, gh_in, right)
    own_out[...] = part_own.astype(BF16)
    own_in_cp = send(24, own_out, own_in, left)
    gh_in_cp.wait_recv()
    own1 = (part_own + gh_in[...].astype(F32)).astype(BF16)

    p_t = jnp.zeros((nv * PAD, 256), F32)
    for s in range(2 * CHIPS):
        p_t += at_targets(s, to_targets(s, own1))
    gh2_out[...] = p_t[:, 128:].astype(BF16)
    gh2_in_cp = send(25, gh2_out, gh2_in, right)
    own_in_cp.wait_recv()
    gh1 = (part_gh + own_in[...].astype(F32)).astype(BF16)
    both1 = jnp.concatenate([own1, gh1], 1)
    p_s = jnp.zeros((nv * PAD, 128), F32)
    for s in range(2 * CHIPS):
        p_s += at_sources(s, to_sources(s, both1))
    gh2_in_cp.wait_recv()
    second = p_s + p_t[:, :128] + gh2_in[...].astype(F32)
    for v in range(nv):
        out_ref[v] = 2.0 * second[v * PAD : v * PAD + orb] - sv[v]
    blocks_out.wait()
    for cp in sent:
        cp.wait_send()


def on_device(node_feat, radial, edge_src, edge_dst, edge_live, w_src, w_dst, w_radial, w_hidden, w_out, start_vectors):
    anywhere = pl.BlockSpec(memory_space=pl.ANY)
    vmem = pl.BlockSpec(memory_space=pltpu.VMEM)
    edges = radial.shape[0]
    nv, orb, atoms = start_vectors.shape
    width = node_feat.shape[1]
    rows = 13 * PAD
    vec = nv * PAD

    def scratch(*shape, dtype=BF16):
        return pltpu.VMEM(shape, dtype)

    return pl.pallas_call(
        kernel,
        out_shape=(
            jax.ShapeDtypeStruct((w_out.shape[0], edges), BF16),
            jax.ShapeDtypeStruct(start_vectors.shape, F32),
        ),
        in_specs=[anywhere, anywhere, vmem, vmem, vmem] + [anywhere] * 6,
        out_specs=(anywhere, vmem),
        scratch_shapes=[
            scratch(atoms, width),
            scratch(atoms, width),
            scratch(CHIPS, edges, radial.shape[1]),
            scratch(*w_src.shape),
            scratch(*w_dst.shape),
            scratch(*w_radial.shape),
            scratch(*w_hidden.shape),
            scratch(*w_out.shape),
            scratch(*start_vectors.shape, dtype=F32),
            scratch(8, 8, 128, dtype=jnp.int32),
            scratch(8, 3 * atoms, edges),
            scratch(8, rows, edges),
            scratch(8, rows, edges, dtype=F32),
            scratch(nv, PAD, edges, dtype=F32),
            scratch(nv, PAD, edges, dtype=F32),
            scratch(8, vec, edges),
            scratch(8, vec, edges),
            scratch(1, vec, atoms),
            scratch(1, vec, atoms),
            scratch(width, 3 * atoms),
            scratch(*w_hidden.shape),
            scratch(width, radial.shape[1]),
            scratch(rows, width),
            scratch(rows, rows),
            scratch(w_out.shape[0], edges),
        ]
        + [scratch(vec, atoms)] * 6
        + [
            pltpu.SemaphoreType.DMA((9,)),
            pltpu.SemaphoreType.DMA((26,)),
            pltpu.SemaphoreType.DMA((26,)),
        ],
        compiler_params=pltpu.CompilerParams(
            collective_id=0, has_side_effects=True, vmem_limit_bytes=40 * 1024 * 1024
        ),
        name="pair_filter",
    )(node_feat, radial, edge_src, edge_dst, edge_live, w_src, w_dst, w_radial, w_hidden, w_out, start_vectors)


def solution(mesh):
    in_specs = (
        P("space", None),
        P(("space", "vec"), None),
        P(("space", "vec")),
        P(("space", "vec")),
        P(("space", "vec")),
        P(),
        P(),
        P(),
        P(),
        P(),
        P("vec", None, "space"),
    )
    out_specs = (P(None, ("space", "vec")), P("vec", None, "space"))
    return jax.shard_map(
        on_device, mesh=mesh, in_specs=in_specs, out_specs=out_specs, check_vma=False
    )
```

```python
import math

import jax
import jax.numpy as jnp
from jax import lax
from jax.experimental import pallas as pl
from jax.experimental.pallas import tpu as pltpu
from jax.sharding import PartitionSpec as P

F32, BF16 = jnp.float32, jnp.bfloat16
MESH = pl.DeviceIdType.MESH
CHIPS = 4
PAD = 16


def silu(v):
    half = 0.5 * v
    return half + half * jnp.tanh(half)


def mm(a, b):
    return jnp.dot(a, b, preferred_element_type=F32)


def mm_nt(a, b):
    return lax.dot_general(a, b, (((1,), (1,)), ((), ())), preferred_element_type=F32)


def transposed(x):
    return x.astype(F32).T.astype(BF16)


def kernel(
    feat_hbm, radial_hbm, src_ref, dst_ref, live_ref, ws_hbm, wd_hbm, wr_hbm, wh_hbm, wo_hbm, sv_hbm,
    blocks_hbm, out_ref,
    feat, ghost, rad, ws, wd, wr, wh, wo, sv,
    info, onehot, ha, hb, xs, xt, pre,
    v_own, v_gh, proj, wht, wrt, wdt, wa, pb, blocks,
    gh_out, own_out, gh_in, own_in, gh2_out, gh2_in,
    local_sem, send_sem, recv_sem,
):
    n_space = lax.axis_size("space")
    d = lax.axis_index("space")
    j = lax.axis_index("vec")
    z, c = j // 2, j % 2
    zk = [z, z + 1 - 2 * (z % 2), (z + 2) % 4, 3 - z]
    left = (lax.rem(d + n_space - 1, n_space), j)
    right = (lax.rem(d + 1, n_space), j)
    same = [(d, zk[k] * 2 + c) for k in range(CHIPS)]
    sibling = (d, z * 2 + 1 - c)
    orb, nv = out_ref.shape[:2]
    layers = wh.shape[0]

    partners = [left, right, sibling] + same[1:]
    barrier = pltpu.get_barrier_semaphore()
    for dev in partners:
        pl.semaphore_signal(barrier, inc=1, device_id=dev, device_id_type=MESH)

    loads = []
    for i, (a, b) in enumerate(
        [(sv_hbm, sv), (feat_hbm, feat), (ws_hbm, ws), (wd_hbm, wd), (wr_hbm, wr), (wh_hbm, wh), (wo_hbm, wo), (radial_hbm, rad.at[0])]
    ):
        cp = pltpu.make_async_copy(a, b, local_sem.at[i])
        cp.start()
        loads.append(cp)

    for row, ref in enumerate((src_ref, dst_ref, live_ref)):
        for h in range(2):
            info[0, 2 * row + h : 2 * row + h + 1, :] = ref[h * 128 : (h + 1) * 128].reshape(1, 128)
    info[0, 6:8, :] = jnp.zeros((2, 128), jnp.int32)
    loads[0].wait()
    start = jnp.concatenate(
        [jnp.concatenate([sv[:, v, :], jnp.zeros((PAD - orb, 128), F32)], 0) for v in range(nv)], 0
    )
    v_own[...] = start.astype(BF16)

    pl.semaphore_wait(barrier, len(partners))

    sent = []

    def send(i, a, b, dev):
        cp = pltpu.make_async_remote_copy(
            src_ref=a, dst_ref=b, send_sem=send_sem.at[i], recv_sem=recv_sem.at[i],
            device_id=dev, device_id_type=MESH,
        )
        cp.start()
        sent.append(cp)
        return cp

    half = pl.ds(pl.multiple_of(c * 64, 64), 64)
    half_in = send(0, feat_hbm.at[half, :], ghost.at[half, :], left)
    vgh_in = send(1, v_own, v_gh, left)
    info_in = [send(1 + k, info.at[0], info.at[k], same[k]) for k in (1, 2, 3)]
    rad_in = [send(4 + k, radial_hbm, rad.at[k], same[k]) for k in (1, 3, 2)]

    def make_onehot(k, r):
        s, t = 2 * k + r, 4 * r + k
        rows = lax.broadcasted_iota(jnp.int32, (256, 128), 0)
        for h in range(2):
            lanes = slice(h * 128, (h + 1) * 128)
            onehot[s, 0:128, lanes] = jnp.where(rows[:128] == info[t, h : h + 1, :], 1.0, 0.0).astype(BF16)
            to = jnp.where(rows == info[t, 2 + h : 3 + h, :], 1.0, 0.0).astype(BF16)
            onehot[s, 128:384, lanes] = to
            if r == 0:
                onehot[s, 384:512, lanes] = to[128:]

    make_onehot(0, 0)
    for cp in info_in:
        cp.wait_recv()
    info_sib = send(8, info.at[0:4], info.at[4:8], sibling)
    for cp in loads[1:]:
        cp.wait()

    wdt[...] = transposed(wd[...])
    for layer in range(layers):
        wht[layer] = transposed(wh[layer])
    wrt[...] = transposed(wr[...])
    rows = lax.broadcasted_iota(jnp.int32, (13 * PAD, 169), 0)
    cols = lax.broadcasted_iota(jnp.int32, (13 * PAD, 169), 1)
    outer, inner = lax.shift_right_logical(rows, 4), lax.bitwise_and(rows, 15)
    spread = jnp.where((inner < orb) & (cols == outer * orb + inner), 1.0, 0.0).astype(BF16)
    wa[...] = mm(spread, wo[...]).astype(BF16)
    rows = lax.broadcasted_iota(jnp.int32, (13 * PAD, 13 * PAD), 0)
    cols = lax.broadcasted_iota(jnp.int32, (13 * PAD, 13 * PAD), 1)
    outer, inner = lax.shift_right_logical(rows, 4), lax.bitwise_and(rows, 15)
    pb[...] = jnp.where((inner < orb) & (cols == inner * PAD + outer), 1.0, 0.0).astype(BF16)

    def halves(x):
        top = x.astype(BF16)
        return top, (x - top.astype(F32)).astype(BF16)

    for n, w in enumerate((transposed(ws[...]), wdt[...])):
        proj[0, :, n * 128 : (n + 1) * 128], proj[1, :, n * 128 : (n + 1) * 128] = halves(mm_nt(w, feat[...]))

    for k in range(1, CHIPS):
        make_onehot(k, 0)

    half_in.wait_recv()
    other_in = send(9, ghost.at[half, :], ghost.at[half, :], sibling)

    for cp in rad_in:
        cp.wait_recv()
    for k in range(CHIPS):
        pre[k] = (
            mm(proj[0], onehot[2 * k, 0:256, :]) + mm(proj[1], onehot[2 * k, 0:256, :]) + mm_nt(wrt[...], rad[k])
        )
    info_sib.wait_recv()
    for k in range(CHIPS):
        make_onehot(k, 1)

    other_in.wait_recv()
    proj[2, :, 0:128], proj[2, :, 128:256] = halves(mm_nt(wdt[...], ghost[...]))

    every = range(CHIPS)
    hidden = [silu(pre[k] + mm(proj[2], onehot[2 * k, 256:512, :])).astype(BF16) for k in every]
    for layer in range(layers):
        hidden = [(hidden[k].astype(F32) + silu(mm(wht[layer], hidden[k]))).astype(BF16) for k in every]
    h_in = []
    for k in every:
        live = jnp.concatenate([info[k, 4:5, :], info[k, 5:6, :]], 1).astype(F32)
        ha[2 * k] = (mm(wa[...], hidden[k]) * live).astype(BF16)
        h_in.append(send(10 + k, ha.at[2 * k], ha.at[2 * k + 1], sibling))
        if k == 0:
            blocks[...] = (mm(wo[...], hidden[0]) * live).astype(BF16)
    blocks_out = pltpu.make_async_copy(blocks, blocks_hbm, local_sem.at[8])
    blocks_out.start()

    def to_targets(s, vec):
        xs[s] = mm(vec, onehot[s, 0:128, :]).reshape(nv, PAD, 256)
        acc = jnp.zeros((nv, PAD, 256), F32)
        for a in range(orb):
            acc += ha[s, a * PAD : (a + 1) * PAD, :].astype(F32)[None] * xs[s, :, a : a + 1, :]
        return mm_nt(acc.reshape(nv * PAD, 256).astype(BF16), onehot[s, 128:384, :])

    def to_sources(s, vec):
        xt[s] = mm(vec, onehot[s, 128:384, :]).reshape(nv, PAD, 256)
        acc = jnp.zeros((nv, PAD, 256), F32)
        for b in range(orb):
            acc += hb[s, b * PAD : (b + 1) * PAD, :][None] * xt[s, :, b : b + 1, :]
        return mm_nt(acc.reshape(nv * PAD, 256).astype(BF16), onehot[s, 0:128, :])

    vgh_in.wait_recv()
    own = v_own[...]
    both = jnp.concatenate([own, v_gh[...]], 1)
    p_t = jnp.zeros((nv * PAD, 256), F32)
    p_s = jnp.zeros((nv * PAD, 128), F32)
    for s in range(0, 2 * CHIPS, 2):
        hb[s] = mm(pb[...], ha[s])
        p_t += to_targets(s, own)
        p_s += to_sources(s, both)
    for cp in h_in:
        cp.wait_recv()
    for s in range(1, 2 * CHIPS, 2):
        p_t += to_targets(s, own)
    part_gh = p_t[:, 128:]
    gh_out[...] = part_gh.astype(BF16)
    gh_in_cp = send(14, gh_out, gh_in, right)
    for s in range(1, 2 * CHIPS, 2):
        hb[s] = mm(pb[...], ha[s])
        p_s += to_sources(s, both)
    part_own = p_s + p_t[:, :128]
    own_out[...] = part_own.astype(BF16)
    own_in_cp = send(15, own_out, own_in, left)

    gh_in_cp.wait_recv()
    own1 = (part_own + gh_in[...].astype(F32)).astype(BF16)
    p_t = jnp.zeros((nv * PAD, 256), F32)
    for s in range(2 * CHIPS):
        p_t += to_targets(s, own1)
    gh2_out[...] = p_t[:, 128:].astype(BF16)
    gh2_in_cp = send(16, gh2_out, gh2_in, right)
    own_in_cp.wait_recv()
    gh1 = (part_gh + own_in[...].astype(F32)).astype(BF16)
    both1 = jnp.concatenate([own1, gh1], 1)
    p_s = jnp.zeros((nv * PAD, 128), F32)
    for s in range(2 * CHIPS):
        p_s += to_sources(s, both1)
    second = 2.0 * (p_s + p_t[:, :128])
    blocks_out.wait()
    for cp in sent:
        cp.wait_send()
    gh2_in_cp.wait_recv()
    second = second + 2.0 * gh2_in[...].astype(F32)
    for v in range(nv):
        out_ref[:, v, :] = second[v * PAD : v * PAD + orb] - sv[:, v, :]


def on_device(node_feat, radial, edge_src, edge_dst, edge_live, w_src, w_dst, w_radial, w_hidden, w_out, start_vectors):
    anywhere = pl.BlockSpec(memory_space=pltpu.HBM)
    vmem = pl.BlockSpec(memory_space=pltpu.VMEM)
    edges = radial.shape[0]
    start_vectors = jnp.transpose(start_vectors, (1, 0, 2))
    orb, nv, atoms = start_vectors.shape
    width = node_feat.shape[1]
    rows = 13 * PAD
    vec = nv * PAD

    def scratch(*shape, dtype=BF16):
        return pltpu.VMEM(shape, dtype)

    pair_blocks, filtered = pl.pallas_call(
        kernel,
        out_shape=(
            jax.ShapeDtypeStruct((w_out.shape[0], edges), BF16),
            jax.ShapeDtypeStruct(start_vectors.shape, F32),
        ),
        in_specs=[anywhere, anywhere, vmem, vmem, vmem] + [anywhere] * 6,
        out_specs=(anywhere, vmem),
        scratch_shapes=[
            scratch(atoms, width),
            scratch(atoms, width),
            scratch(CHIPS, edges, radial.shape[1]),
            scratch(*w_src.shape),
            scratch(*w_dst.shape),
            scratch(*w_radial.shape),
            scratch(*w_hidden.shape),
            scratch(*w_out.shape),
            scratch(*start_vectors.shape, dtype=F32),
            scratch(8, 8, 128, dtype=jnp.int32),
            scratch(8, 4 * atoms, edges),
            scratch(8, rows, edges),
            scratch(8, rows, edges, dtype=F32),
            scratch(8, nv, PAD, edges, dtype=F32),
            scratch(8, nv, PAD, edges, dtype=F32),
            scratch(CHIPS, width, edges, dtype=F32),
            scratch(vec, atoms),
            scratch(vec, atoms),
            scratch(3, width, 2 * atoms),
            scratch(*w_hidden.shape),
            scratch(width, radial.shape[1]),
            scratch(*w_dst.shape),
            scratch(rows, width),
            scratch(rows, rows),
            scratch(w_out.shape[0], edges),
        ]
        + [scratch(vec, atoms)] * 6
        + [
            pltpu.SemaphoreType.DMA((9,)),
            pltpu.SemaphoreType.DMA((17,)),
            pltpu.SemaphoreType.DMA((17,)),
        ],
        compiler_params=pltpu.CompilerParams(
            collective_id=0, has_side_effects=True, vmem_limit_bytes=60 * 1024 * 1024
        ),
        name="pair_filter",
    )(node_feat, radial, edge_src, edge_dst, edge_live, w_src, w_dst, w_radial, w_hidden, w_out, start_vectors)
    return pair_blocks, jnp.transpose(filtered, (1, 0, 2))


def solution(mesh):
    in_specs = (
        P("space", None),
        P(("space", "vec"), None),
        P(("space", "vec")),
        P(("space", "vec")),
        P(("space", "vec")),
        P(),
        P(),
        P(),
        P(),
        P(),
        P("vec", None, "space"),
    )
    out_specs = (P(None, ("space", "vec")), P("vec", None, "space"))
    return jax.shard_map(
        on_device, mesh=mesh, in_specs=in_specs, out_specs=out_specs, check_vma=False
    )
```

```python
import math

import jax
import jax.numpy as jnp
from jax import lax
from jax.experimental import pallas as pl
from jax.experimental.pallas import tpu as pltpu
from jax.sharding import PartitionSpec as P

F32, BF16 = jnp.float32, jnp.bfloat16
MESH = pl.DeviceIdType.MESH
CHIPS = 4
PAD = 16


def silu(v):
    half = 0.5 * v
    return half + half * jnp.tanh(half)


def mm(a, b):
    return jnp.dot(a, b, preferred_element_type=F32)


def mm_nt(a, b):
    return lax.dot_general(a, b, (((1,), (1,)), ((), ())), preferred_element_type=F32)


def transposed(x):
    return x.astype(F32).T.astype(BF16)


def kernel(
    feat_hbm, radial_hbm, src_hbm, dst_hbm, live_hbm, ws_hbm, wd_hbm, wr_hbm, wh_hbm, wo_hbm, sv_hbm,
    blocks_ref, out_ref,
    src_ref, dst_ref, live_ref,
    feat, ghost, rad, ws, wd, wr, wh, wo, sv,
    info, onehot, ha, hb, xs, xt, pre,
    v_own, v_gh, proj, wht, wrt, wdt, wa, pb,
    gh_out, own_out, gh_in, own_in, gh2_out, gh2_in,
    local_sem, send_sem, recv_sem, ready_sem,
):
    n_space = lax.axis_size("space")
    d = lax.axis_index("space")
    j = lax.axis_index("vec")
    z, c = j // 2, j % 2
    zk = [z, z + 1 - 2 * (z % 2), (z + 2) % 4, 3 - z]
    before, after = lax.rem(d + n_space - 1, n_space), lax.rem(d + 1, n_space)
    left, right = (before, j), (after, j)
    same = [(d, zk[k] * 2 + c) for k in range(CHIPS)]
    sibling = (d, z * 2 + 1 - c)
    feat_from = (after, (z + (d % 4) // 3 * (3 - 2 * z)) * 2 + 1)
    feat_to = (before, (z + (before % 4) // 3 * (3 - 2 * z)) * 2 + 1)
    orb, nv = out_ref.shape[:2]
    layers = wh.shape[0]

    barrier = pltpu.get_barrier_semaphore()

    def hello(dev):
        pl.semaphore_signal(barrier, inc=1, device_id=dev, device_id_type=MESH)

    @pl.when(c == 1)
    def _():
        hello(feat_from)
        hello(sibling)

    for nb in (after, before):
        hello((nb, z * 2 + 1))
    for k in range(1, CHIPS):
        hello((d, zk[k] * 2))

    loads = []
    for i, (a, b) in enumerate(
        [(sv_hbm, sv), (feat_hbm, feat), (ws_hbm, ws), (wd_hbm, wd), (wr_hbm, wr), (wh_hbm, wh), (wo_hbm, wo), (radial_hbm, rad.at[0]), (src_hbm, src_ref), (dst_hbm, dst_ref), (live_hbm, live_ref)]
    ):
        cp = pltpu.make_async_copy(a, b, local_sem.at[i])
        cp.start()
        loads.append(cp)

    for cp in loads[8:]:
        cp.wait()
    for row, ref in enumerate((src_ref, dst_ref, live_ref)):
        for h in range(2):
            info[0, 2 * row + h : 2 * row + h + 1, :] = ref[h * 128 : (h + 1) * 128].reshape(1, 128)
    info[0, 6:8, :] = jnp.zeros((2, 128), jnp.int32)
    loads[0].wait()
    start = jnp.concatenate(
        [jnp.concatenate([sv[:, v, :], jnp.zeros((PAD - orb, 128), F32)], 0) for v in range(nv)], 0
    )
    v_own[...] = start.astype(BF16)

    def tell_other_core():
        pl.semaphore_signal(ready_sem, inc=1, device_id=sibling, device_id_type=MESH)

    @pl.when(c == 0)
    def _():
        pl.semaphore_wait(barrier, 7)
        tell_other_core()

    @pl.when(c == 1)
    def _():
        pl.semaphore_wait(ready_sem, 1)

    sent = []

    def copy_to(i, a, b, dev):
        return pltpu.make_async_remote_copy(
            src_ref=a, dst_ref=b, send_sem=send_sem.at[i], recv_sem=recv_sem.at[i],
            device_id=dev, device_id_type=MESH,
        )

    def send(i, a, b, dev):
        cp = copy_to(i, a, b, dev)
        cp.start()
        sent.append(cp)
        return cp

    info_in = [send(k, info.at[0], info.at[k], same[k]) for k in (1, 2, 3)]
    rad_in = [send(3 + k, radial_hbm, rad.at[k], same[k]) for k in (1, 3, 2)]

    def make_onehot(k, r):
        s, t = 2 * k + r, 4 * r + k
        rows = lax.broadcasted_iota(jnp.int32, (256, 128), 0)
        for h in range(2):
            lanes = slice(h * 128, (h + 1) * 128)
            onehot[s, 0:128, lanes] = jnp.where(rows[:128] == info[t, h : h + 1, :], 1.0, 0.0).astype(BF16)
            to = jnp.where(rows == info[t, 2 + h : 3 + h, :], 1.0, 0.0).astype(BF16)
            onehot[s, 128:384, lanes] = to
            if r == 0:
                onehot[s, 384:512, lanes] = to[128:]

    make_onehot(0, 0)
    for cp in info_in:
        cp.wait_recv()
    info_sib = send(8, info.at[0:4], info.at[4:8], sibling)
    for cp in loads[1:8]:
        cp.wait()

    wdt[...] = transposed(wd[...])
    for layer in range(layers):
        wht[layer] = transposed(wh[layer])
    wrt[...] = transposed(wr[...])
    rows = lax.broadcasted_iota(jnp.int32, (13 * PAD, 169), 0)
    cols = lax.broadcasted_iota(jnp.int32, (13 * PAD, 169), 1)
    outer, inner = lax.shift_right_logical(rows, 4), lax.bitwise_and(rows, 15)
    spread = jnp.where((inner < orb) & (cols == outer * orb + inner), 1.0, 0.0).astype(BF16)
    wa[...] = mm(spread, wo[...]).astype(BF16)
    rows = lax.broadcasted_iota(jnp.int32, (13 * PAD, 13 * PAD), 0)
    cols = lax.broadcasted_iota(jnp.int32, (13 * PAD, 13 * PAD), 1)
    outer, inner = lax.shift_right_logical(rows, 4), lax.bitwise_and(rows, 15)
    pb[...] = jnp.where((inner < orb) & (cols == inner * PAD + outer), 1.0, 0.0).astype(BF16)

    def halves(x):
        top = x.astype(BF16)
        return top, (x - top.astype(F32)).astype(BF16)

    for n, w in enumerate((transposed(ws[...]), wdt[...])):
        proj[0, :, n * 128 : (n + 1) * 128], proj[1, :, n * 128 : (n + 1) * 128] = halves(mm_nt(w, feat[...]))

    for k in range(1, CHIPS):
        make_onehot(k, 0)

    feat_cp = copy_to(0, feat_hbm, ghost, feat_to)
    pass_on = copy_to(9, ghost, ghost, sibling)

    @pl.when(c == 1)
    def _():
        pl.semaphore_wait(barrier, 5)
        feat_cp.start()
        tell_other_core()

    @pl.when(c == 0)
    def _():
        pl.semaphore_wait(ready_sem, 1)

    vgh_in = send(7, v_own, v_gh, left)

    for cp in rad_in:
        cp.wait_recv()
    for k in range(CHIPS):
        pre[k] = (
            mm(proj[0], onehot[2 * k, 0:256, :]) + mm(proj[1], onehot[2 * k, 0:256, :]) + mm_nt(wrt[...], rad[k])
        )
    info_sib.wait_recv()
    for k in range(CHIPS):
        make_onehot(k, 1)

    @pl.when(c == 1)
    def _():
        feat_cp.wait_recv()
        pass_on.start()

    @pl.when(c == 0)
    def _():
        pass_on.wait_recv()

    proj[2, :, 0:128], proj[2, :, 128:256] = halves(mm_nt(wdt[...], ghost[...]))

    every = range(CHIPS)
    hidden = [silu(pre[k] + mm(proj[2], onehot[2 * k, 256:512, :])).astype(BF16) for k in every]
    for layer in range(layers):
        hidden = [(hidden[k].astype(F32) + silu(mm(wht[layer], hidden[k]))).astype(BF16) for k in every]
    h_in = []
    for k in every:
        live = jnp.concatenate([info[k, 4:5, :], info[k, 5:6, :]], 1).astype(F32)
        ha[2 * k] = (mm(wa[...], hidden[k]) * live).astype(BF16)
        h_in.append(send(10 + k, ha.at[2 * k], ha.at[2 * k + 1], sibling))
        if k == 0:
            blocks_ref[...] = (mm(wo[...], hidden[0]) * live).astype(BF16)

    def to_targets(s, vec):
        xs[s] = mm(vec, onehot[s, 0:128, :]).reshape(nv, PAD, 256)
        acc = jnp.zeros((nv, PAD, 256), F32)
        for a in range(orb):
            acc += ha[s, a * PAD : (a + 1) * PAD, :].astype(F32)[None] * xs[s, :, a : a + 1, :]
        return mm_nt(acc.reshape(nv * PAD, 256).astype(BF16), onehot[s, 128:384, :])

    def to_sources(s, vec):
        xt[s] = mm(vec, onehot[s, 128:384, :]).reshape(nv, PAD, 256)
        acc = jnp.zeros((nv, PAD, 256), F32)
        for b in range(orb):
            acc += hb[s, b * PAD : (b + 1) * PAD, :][None] * xt[s, :, b : b + 1, :]
        return mm_nt(acc.reshape(nv * PAD, 256).astype(BF16), onehot[s, 0:128, :])

    vgh_in.wait_recv()
    own = v_own[...]
    both = jnp.concatenate([own, v_gh[...]], 1)
    p_t = jnp.zeros((nv * PAD, 256), F32)
    p_s = jnp.zeros((nv * PAD, 128), F32)
    for s in range(0, 2 * CHIPS, 2):
        hb[s] = mm(pb[...], ha[s])
        p_t += to_targets(s, own)
        p_s += to_sources(s, both)
    for cp in h_in:
        cp.wait_recv()
    for s in range(1, 2 * CHIPS, 2):
        p_t += to_targets(s, own)
    part_gh = p_t[:, 128:]
    gh_out[...] = part_gh.astype(BF16)
    gh_in_cp = send(14, gh_out, gh_in, right)
    for s in range(1, 2 * CHIPS, 2):
        hb[s] = mm(pb[...], ha[s])
        p_s += to_sources(s, both)
    part_own = p_s + p_t[:, :128]
    own_out[...] = part_own.astype(BF16)
    own_in_cp = send(15, own_out, own_in, left)

    gh_in_cp.wait_recv()
    own1 = (part_own + gh_in[...].astype(F32)).astype(BF16)
    p_t = jnp.zeros((nv * PAD, 256), F32)
    for s in range(2 * CHIPS):
        p_t += to_targets(s, own1)
    gh2_out[...] = p_t[:, 128:].astype(BF16)
    gh2_in_cp = send(16, gh2_out, gh2_in, right)
    own_in_cp.wait_recv()
    gh1 = (part_gh + own_in[...].astype(F32)).astype(BF16)
    both1 = jnp.concatenate([own1, gh1], 1)
    p_s = jnp.zeros((nv * PAD, 128), F32)
    for s in range(2 * CHIPS):
        p_s += to_sources(s, both1)
    second = 2.0 * (p_s + p_t[:, :128])
    for cp in sent:
        cp.wait_send()

    @pl.when(c == 1)
    def _():
        feat_cp.wait_send()
        pass_on.wait_send()

    gh2_in_cp.wait_recv()
    second = second + 2.0 * gh2_in[...].astype(F32)
    for v in range(nv):
        out_ref[:, v, :] = second[v * PAD : v * PAD + orb] - sv[:, v, :]


def on_device(node_feat, radial, edge_src, edge_dst, edge_live, w_src, w_dst, w_radial, w_hidden, w_out, start_vectors):
    anywhere = pl.BlockSpec(memory_space=pltpu.HBM)
    vmem = pl.BlockSpec(memory_space=pltpu.VMEM)
    edges = radial.shape[0]
    start_vectors = jnp.transpose(start_vectors, (1, 0, 2))
    orb, nv, atoms = start_vectors.shape
    width = node_feat.shape[1]
    rows = 13 * PAD
    vec = nv * PAD

    def scratch(*shape, dtype=BF16):
        return pltpu.VMEM(shape, dtype)

    pair_blocks, filtered = pl.pallas_call(
        kernel,
        out_shape=(
            pltpu.VMEM((w_out.shape[0], edges), BF16),
            pltpu.VMEM(start_vectors.shape, F32),
        ),
        in_specs=[anywhere] * 11,
        out_specs=(vmem, vmem),
        scratch_shapes=[scratch(edges, dtype=jnp.int32)] * 3
        + [
            scratch(atoms, width),
            scratch(atoms, width),
            scratch(CHIPS, edges, radial.shape[1]),
            scratch(*w_src.shape),
            scratch(*w_dst.shape),
            scratch(*w_radial.shape),
            scratch(*w_hidden.shape),
            scratch(*w_out.shape),
            scratch(*start_vectors.shape, dtype=F32),
            scratch(8, 8, 128, dtype=jnp.int32),
            scratch(8, 4 * atoms, edges),
            scratch(8, rows, edges),
            scratch(8, rows, edges, dtype=F32),
            scratch(8, nv, PAD, edges, dtype=F32),
            scratch(8, nv, PAD, edges, dtype=F32),
            scratch(CHIPS, width, edges, dtype=F32),
            scratch(vec, atoms),
            scratch(vec, atoms),
            scratch(3, width, 2 * atoms),
            scratch(*w_hidden.shape),
            scratch(width, radial.shape[1]),
            scratch(*w_dst.shape),
            scratch(rows, width),
            scratch(rows, rows),
        ]
        + [scratch(vec, atoms)] * 6
        + [
            pltpu.SemaphoreType.DMA((11,)),
            pltpu.SemaphoreType.DMA((17,)),
            pltpu.SemaphoreType.DMA((17,)),
            pltpu.SemaphoreType.REGULAR,
        ],
        compiler_params=pltpu.CompilerParams(
            collective_id=0, has_side_effects=True, vmem_limit_bytes=60 * 1024 * 1024
        ),
        name="pair_filter",
    )(node_feat, radial, edge_src, edge_dst, edge_live, w_src, w_dst, w_radial, w_hidden, w_out, start_vectors)
    return pair_blocks, jnp.transpose(filtered, (1, 0, 2))


def solution(mesh):
    in_specs = (
        P("space", None),
        P(("space", "vec"), None),
        P(("space", "vec")),
        P(("space", "vec")),
        P(("space", "vec")),
        P(),
        P(),
        P(),
        P(),
        P(),
        P("vec", None, "space"),
    )
    out_specs = (P(None, ("space", "vec")), P("vec", None, "space"))
    return jax.shard_map(
        on_device, mesh=mesh, in_specs=in_specs, out_specs=out_specs, check_vma=False
    )
```

```python
import math

import jax
import jax.numpy as jnp
from jax import lax
from jax.experimental import pallas as pl
from jax.experimental.pallas import tpu as pltpu
from jax.sharding import PartitionSpec as P

F32, BF16 = jnp.float32, jnp.bfloat16
MESH = pl.DeviceIdType.MESH
CHIPS = 4
PAD = 16


def silu(v):
    half = 0.5 * v
    return half + half * jnp.tanh(half)


def mm(a, b):
    return jnp.dot(a, b, preferred_element_type=F32)


def mm_nt(a, b):
    return lax.dot_general(a, b, (((1,), (1,)), ((), ())), preferred_element_type=F32)


def transposed(x):
    return x.astype(F32).T.astype(BF16)


def kernel(
    feat_hbm, radial_hbm, src_hbm, dst_hbm, live_hbm, ws_hbm, wd_hbm, wr_hbm, wh_hbm, wo_hbm, sv_hbm,
    blocks_ref, out_ref,
    src_ref, dst_ref, live_ref,
    feat, ghost, via, rad, ws, wd, wr, wh, wo, sv,
    info, onehot, ha, hf, hb, xs, xt, pre,
    v_own, v_gh, proj, wht, wrt, wdt, wa, pb,
    gh_out, own_out, gh_in, own_in, gh2_out, gh2_in,
    local_sem, send_sem, recv_sem, ready_sem,
):
    n_space = lax.axis_size("space")
    d = lax.axis_index("space")
    j = lax.axis_index("vec")
    z, c = j // 2, j % 2
    zk = [z, z + 1 - 2 * (z % 2), (z + 2) % 4, 3 - z]
    before, after = lax.rem(d + n_space - 1, n_space), lax.rem(d + 1, n_space)
    left, right = (before, j), (after, j)
    same = [(d, zk[k] * 2 + c) for k in range(CHIPS)]
    sibling = (d, z * 2 + 1 - c)
    at_end, at_start = d % 4 == 3, d % 4 == 0
    flip = d + 4 - 8 * (d // 4 % 2)
    flip_before = before + 4 - 8 * (before // 4 % 2)
    flip_after = lax.rem(flip + 1, n_space)
    orb, nv = out_ref.shape[:2]
    layers = wh.shape[0]

    barrier = pltpu.get_barrier_semaphore()

    def hello(dev):
        pl.semaphore_signal(barrier, inc=1, device_id=dev, device_id_type=MESH)

    @pl.when((c == 1) & at_end)
    def _():
        hello((flip, (3 - z) * 2))
        hello((flip_after, z * 2))

    @pl.when((c == 1) & jnp.logical_not(at_end))
    def _():
        hello((after, z * 2))

    for nb in (after, before):
        hello((nb, z * 2 + 1))
    for k in range(1, CHIPS):
        hello((d, zk[k] * 2))

    @pl.when(c == 1)
    def _():
        hello(sibling)

    loads = []
    for i, (a, b) in enumerate(
        [(sv_hbm, sv), (feat_hbm, feat), (ws_hbm, ws), (wd_hbm, wd), (wr_hbm, wr), (wh_hbm, wh), (wo_hbm, wo), (radial_hbm, rad.at[0]), (src_hbm, src_ref), (dst_hbm, dst_ref), (live_hbm, live_ref)]
    ):
        cp = pltpu.make_async_copy(a, b, local_sem.at[i])
        cp.start()
        loads.append(cp)

    for cp in loads[7:] + loads[1:2]:
        cp.wait()
    for row, ref in enumerate((src_ref, dst_ref, live_ref)):
        for h in range(2):
            info[0, 2 * row + h : 2 * row + h + 1, :] = ref[h * 128 : (h + 1) * 128].reshape(1, 128)
    info[0, 6:8, :] = jnp.zeros((2, 128), jnp.int32)
    loads[0].wait()
    start = jnp.concatenate(
        [jnp.concatenate([sv[:, v, :], jnp.zeros((PAD - orb, 128), F32)], 0) for v in range(nv)], 0
    )
    v_own[...] = start.astype(BF16)

    def tell_other_core():
        pl.semaphore_signal(ready_sem, inc=1, device_id=sibling, device_id_type=MESH)

    @pl.when(c == 0)
    def _():
        @pl.when(at_end)
        def _():
            pl.semaphore_wait(barrier, 9)

        @pl.when(jnp.logical_not(at_end))
        def _():
            pl.semaphore_wait(barrier, 8)

        tell_other_core()

    @pl.when(c == 1)
    def _():
        pl.semaphore_wait(ready_sem, 1)

    sent = []

    def copy_to(i, a, b, dev, own=None):
        return pltpu.make_async_remote_copy(
            src_ref=a, dst_ref=b, send_sem=send_sem.at[i if own is None else own], recv_sem=recv_sem.at[i],
            device_id=dev, device_id_type=MESH,
        )

    def send(i, a, b, dev):
        cp = copy_to(i, a, b, dev)
        cp.start()
        sent.append(cp)
        return cp

    info_in = [send(k, info.at[0], info.at[k], same[k]) for k in (1, 2, 3)]
    feat_near = copy_to(0, feat, ghost, (before, z * 2 + 1))
    feat_far = copy_to(17, feat, via, (flip_before, z * 2 + 1))
    feat_via = copy_to(0, via, ghost, (flip, (3 - z) * 2 + 1), 18)
    pass_on = copy_to(9, ghost, ghost, sibling)

    @pl.when((c == 1) & at_start)
    def _():
        feat_far.start()

    @pl.when((c == 1) & jnp.logical_not(at_start))
    def _():
        feat_near.start()

    rad_in = [send(3 + k, rad.at[0], rad.at[k], same[k]) for k in (1, 3, 2)]

    @pl.when((c == 1) & at_end & (flip > d))
    def _():
        feat_far.wait_recv()
        feat_via.start()

    def make_onehot(k, r):
        s, t = 2 * k + r, 4 * r + k
        rows = lax.broadcasted_iota(jnp.int32, (256, 128), 0)
        for h in range(2):
            lanes = slice(h * 128, (h + 1) * 128)
            onehot[s, 0:128, lanes] = jnp.where(rows[:128] == info[t, h : h + 1, :], 1.0, 0.0).astype(BF16)
            to = jnp.where(rows == info[t, 2 + h : 3 + h, :], 1.0, 0.0).astype(BF16)
            onehot[s, 128:384, lanes] = to
            if r == 0:
                onehot[s, 384:512, lanes] = to[128:]

    make_onehot(0, 0)
    for cp in info_in:
        cp.wait_recv()
    info_sib = send(8, info.at[0:4], info.at[4:8], sibling)
    for cp in loads[2:7]:
        cp.wait()

    wdt[...] = transposed(wd[...])
    for layer in range(layers):
        wht[layer] = transposed(wh[layer])
    wrt[...] = transposed(wr[...])
    rows = lax.broadcasted_iota(jnp.int32, (13 * PAD, 169), 0)
    cols = lax.broadcasted_iota(jnp.int32, (13 * PAD, 169), 1)
    outer, inner = lax.shift_right_logical(rows, 4), lax.bitwise_and(rows, 15)
    spread = jnp.where((inner < orb) & (cols == outer * orb + inner), 1.0, 0.0).astype(BF16)
    wa[...] = mm(spread, wo[...]).astype(BF16)
    rows = lax.broadcasted_iota(jnp.int32, (13 * PAD, 13 * PAD), 0)
    cols = lax.broadcasted_iota(jnp.int32, (13 * PAD, 13 * PAD), 1)
    outer, inner = lax.shift_right_logical(rows, 4), lax.bitwise_and(rows, 15)
    pb[...] = jnp.where((inner < orb) & (cols == inner * PAD + outer), 1.0, 0.0).astype(BF16)

    def halves(x):
        top = x.astype(BF16)
        return top, (x - top.astype(F32)).astype(BF16)

    for n, w in enumerate((transposed(ws[...]), wdt[...])):
        proj[0, :, n * 128 : (n + 1) * 128], proj[1, :, n * 128 : (n + 1) * 128] = halves(mm_nt(w, feat[...]))

    for k in range(1, CHIPS):
        make_onehot(k, 0)

    @pl.when(c == 1)
    def _():
        pl.semaphore_wait(barrier, 4)
        tell_other_core()

    @pl.when(c == 0)
    def _():
        pl.semaphore_wait(ready_sem, 1)

    vgh_in = send(7, v_own, v_gh, left)

    @pl.when((c == 1) & at_end & (flip < d))
    def _():
        feat_far.wait_recv()
        feat_via.start()

    info_sib.wait_recv()
    for k in range(CHIPS):
        make_onehot(k, 1)
    arrived = dict(zip((1, 3, 2), rad_in))
    for k in (0, 1, 3, 2):
        if k:
            arrived[k].wait_recv()
        pre[k] = (
            mm(proj[0], onehot[2 * k, 0:256, :]) + mm(proj[1], onehot[2 * k, 0:256, :]) + mm_nt(wrt[...], rad[k])
        )

    @pl.when(c == 1)
    def _():
        feat_near.wait_recv()
        pass_on.start()

    @pl.when(c == 0)
    def _():
        pass_on.wait_recv()

    proj[2, :, 0:128], proj[2, :, 128:256] = halves(mm_nt(wdt[...], ghost[...]))

    every = range(CHIPS)
    hidden = [silu(pre[k] + mm(proj[2], onehot[2 * k, 256:512, :])).astype(BF16) for k in every]
    for layer in range(layers):
        hidden = [(hidden[k].astype(F32) + silu(mm(wht[layer], hidden[k]))).astype(BF16) for k in every]
    h_in = []
    for k in every:
        live = jnp.concatenate([info[k, 4:5, :], info[k, 5:6, :]], 1).astype(F32)
        ha[2 * k] = (mm(wa[...], hidden[k]) * live).astype(BF16)
        h_in.append(send(10 + k, ha.at[2 * k], ha.at[2 * k + 1], sibling))
        if k == 0:
            blocks_ref[...] = (mm(wo[...], hidden[0]) * live).astype(BF16)

    def to_targets(s, vec, h):
        xs[s] = mm(vec, onehot[s, 0:128, :]).reshape(nv, PAD, 256)
        acc = jnp.zeros((nv, PAD, 256), F32)
        for a in range(orb):
            acc += h[s, a * PAD : (a + 1) * PAD, :].astype(F32)[None] * xs[s, :, a : a + 1, :]
        return mm_nt(acc.reshape(nv * PAD, 256).astype(BF16), onehot[s, 128:384, :])

    def to_sources(s, vec):
        xt[s] = mm(vec, onehot[s, 128:384, :]).reshape(nv, PAD, 256)
        acc = jnp.zeros((nv, PAD, 256), F32)
        for b in range(orb):
            acc += hb[s, b * PAD : (b + 1) * PAD, :][None] * xt[s, :, b : b + 1, :]
        return mm_nt(acc.reshape(nv * PAD, 256).astype(BF16), onehot[s, 0:128, :])

    own = v_own[...]
    p_t = jnp.zeros((nv * PAD, 256), F32)
    p_s = jnp.zeros((nv * PAD, 128), F32)
    for s in range(0, 2 * CHIPS, 2):
        p_t += to_targets(s, own, ha)
    for cp in h_in:
        cp.wait_recv()
    for s in range(1, 2 * CHIPS, 2):
        p_t += to_targets(s, own, ha)
    part_gh = p_t[:, 128:]
    gh_out[...] = part_gh.astype(BF16)
    gh_in_cp = send(14, gh_out, gh_in, right)
    vgh_in.wait_recv()
    both = jnp.concatenate([own, v_gh[...]], 1)
    for s in range(2 * CHIPS):
        hb[s] = mm(pb[...], ha[s])
        p_s += to_sources(s, both)
    part_own = p_s + p_t[:, :128]
    own_out[...] = part_own.astype(BF16)
    own_in_cp = send(15, own_out, own_in, left)

    for s in range(2 * CHIPS):
        hf[s] = ha[s].astype(F32)
    gh_in_cp.wait_recv()
    own1 = (part_own + gh_in[...].astype(F32)).astype(BF16)
    p_t = jnp.zeros((nv * PAD, 256), F32)
    for s in range(2 * CHIPS):
        p_t += to_targets(s, own1, hf)
    gh2_out[...] = p_t[:, 128:].astype(BF16)
    gh2_in_cp = send(16, gh2_out, gh2_in, right)
    own_in_cp.wait_recv()
    gh1 = (part_gh + own_in[...].astype(F32)).astype(BF16)
    both1 = jnp.concatenate([own1, gh1], 1)
    p_s = jnp.zeros((nv * PAD, 128), F32)
    for s in range(2 * CHIPS):
        p_s += to_sources(s, both1)
    second = 2.0 * (p_s + p_t[:, :128])
    for cp in sent:
        cp.wait_send()

    @pl.when(c == 1)
    def _():
        pass_on.wait_send()

    @pl.when((c == 1) & at_start)
    def _():
        feat_far.wait_send()

    @pl.when((c == 1) & jnp.logical_not(at_start))
    def _():
        feat_near.wait_send()

    @pl.when((c == 1) & at_end)
    def _():
        feat_via.wait_send()

    gh2_in_cp.wait_recv()
    second = second + 2.0 * gh2_in[...].astype(F32)
    for v in range(nv):
        out_ref[:, v, :] = second[v * PAD : v * PAD + orb] - sv[:, v, :]


def on_device(node_feat, radial, edge_src, edge_dst, edge_live, w_src, w_dst, w_radial, w_hidden, w_out, start_vectors):
    anywhere = pl.BlockSpec(memory_space=pltpu.HBM)
    vmem = pl.BlockSpec(memory_space=pltpu.VMEM)
    edges = radial.shape[0]
    start_vectors = jnp.transpose(start_vectors, (1, 0, 2))
    orb, nv, atoms = start_vectors.shape
    width = node_feat.shape[1]
    rows = 13 * PAD
    vec = nv * PAD

    def scratch(*shape, dtype=BF16):
        return pltpu.VMEM(shape, dtype)

    pair_blocks, filtered = pl.pallas_call(
        kernel,
        out_shape=(
            pltpu.VMEM((w_out.shape[0], edges), BF16),
            pltpu.VMEM(start_vectors.shape, F32),
        ),
        in_specs=[anywhere] * 11,
        out_specs=(vmem, vmem),
        scratch_shapes=[scratch(edges, dtype=jnp.int32)] * 3
        + [
            scratch(atoms, width),
            scratch(atoms, width),
            scratch(atoms, width),
            scratch(CHIPS, edges, radial.shape[1]),
            scratch(*w_src.shape),
            scratch(*w_dst.shape),
            scratch(*w_radial.shape),
            scratch(*w_hidden.shape),
            scratch(*w_out.shape),
            scratch(*start_vectors.shape, dtype=F32),
            scratch(8, 8, 128, dtype=jnp.int32),
            scratch(8, 4 * atoms, edges),
            scratch(8, rows, edges),
            scratch(8, rows, edges, dtype=F32),
            scratch(8, rows, edges, dtype=F32),
            scratch(8, nv, PAD, edges, dtype=F32),
            scratch(8, nv, PAD, edges, dtype=F32),
            scratch(CHIPS, width, edges, dtype=F32),
            scratch(vec, atoms),
            scratch(vec, atoms),
            scratch(3, width, 2 * atoms),
            scratch(*w_hidden.shape),
            scratch(width, radial.shape[1]),
            scratch(*w_dst.shape),
            scratch(rows, width),
            scratch(rows, rows),
        ]
        + [scratch(vec, atoms)] * 6
        + [
            pltpu.SemaphoreType.DMA((11,)),
            pltpu.SemaphoreType.DMA((19,)),
            pltpu.SemaphoreType.DMA((19,)),
            pltpu.SemaphoreType.REGULAR,
        ],
        compiler_params=pltpu.CompilerParams(
            collective_id=0, has_side_effects=True, vmem_limit_bytes=60 * 1024 * 1024
        ),
        name="pair_filter",
    )(node_feat, radial, edge_src, edge_dst, edge_live, w_src, w_dst, w_radial, w_hidden, w_out, start_vectors)
    return pair_blocks, jnp.transpose(filtered, (1, 0, 2))


def solution(mesh):
    in_specs = (
        P("space", None),
        P(("space", "vec"), None),
        P(("space", "vec")),
        P(("space", "vec")),
        P(("space", "vec")),
        P(),
        P(),
        P(),
        P(),
        P(),
        P("vec", None, "space"),
    )
    out_specs = (P(None, ("space", "vec")), P("vec", None, "space"))
    return jax.shard_map(
        on_device, mesh=mesh, in_specs=in_specs, out_specs=out_specs, check_vma=False
    )
```

```python
import math

import jax
import jax.numpy as jnp
from jax import lax
from jax.experimental import pallas as pl
from jax.experimental.pallas import tpu as pltpu
from jax.sharding import PartitionSpec as P

F32, BF16 = jnp.float32, jnp.bfloat16
MESH = pl.DeviceIdType.MESH
CHIPS = 4
PAD = 16


def silu(v):
    half = 0.5 * v
    return half + half * jnp.tanh(half)


def mm(a, b):
    return jnp.dot(a, b, preferred_element_type=F32)


def mm_nt(a, b):
    return lax.dot_general(a, b, (((1,), (1,)), ((), ())), preferred_element_type=F32)


def transposed(x):
    return x.astype(F32).T.astype(BF16)


def kernel(
    feat_hbm, radial_hbm, src_hbm, dst_hbm, live_hbm, ws_hbm, wd_hbm, wr_hbm, wh_hbm, wo_hbm, sv_hbm,
    blocks_ref, out_ref,
    src_ref, dst_ref, live_ref,
    feat, ghost, via, rad, ws, wd, wr, wh, wo, sv,
    info, onehot, ha, hf, hb, xs, xt,
    v_own, v_gh, proj, wht, wrt, wdt, wa, pb,
    gh_out, own_out, gh_in, own_in, gh2_out, gh2_in,
    local_sem, send_sem, recv_sem, ready_sem,
):
    n_space = lax.axis_size("space")
    d = lax.axis_index("space")
    j = lax.axis_index("vec")
    z, c = j // 2, j % 2
    zk = [z, z + 1 - 2 * (z % 2), (z + 2) % 4, 3 - z]
    before, after = lax.rem(d + n_space - 1, n_space), lax.rem(d + 1, n_space)
    left, right = (before, j), (after, j)
    same = [(d, zk[k] * 2 + c) for k in range(CHIPS)]
    sibling = (d, z * 2 + 1 - c)
    at_end, at_start = d % 4 == 3, d % 4 == 0
    flip = d + 4 - 8 * (d // 4 % 2)
    flip_before = before + 4 - 8 * (before // 4 % 2)
    flip_after = lax.rem(flip + 1, n_space)
    orb, nv = out_ref.shape[:2]
    layers = wh.shape[0]

    barrier = pltpu.get_barrier_semaphore()

    def hello(dev):
        pl.semaphore_signal(barrier, inc=1, device_id=dev, device_id_type=MESH)

    @pl.when((c == 1) & at_end)
    def _():
        hello((flip, (3 - z) * 2))
        hello((flip_after, z * 2))

    @pl.when((c == 1) & jnp.logical_not(at_end))
    def _():
        hello((after, z * 2))

    for nb in (after, before):
        hello((nb, z * 2 + 1))
    for k in range(1, CHIPS):
        hello((d, zk[k] * 2))

    @pl.when(c == 1)
    def _():
        hello(sibling)

    loads = []
    for i, (a, b) in enumerate(
        [(sv_hbm, sv), (feat_hbm, feat), (ws_hbm, ws), (wd_hbm, wd), (wr_hbm, wr), (wh_hbm, wh), (wo_hbm, wo), (radial_hbm, rad.at[0]), (src_hbm, src_ref), (dst_hbm, dst_ref), (live_hbm, live_ref)]
    ):
        cp = pltpu.make_async_copy(a, b, local_sem.at[i])
        cp.start()
        loads.append(cp)

    for cp in loads[7:] + loads[1:2]:
        cp.wait()
    for row, ref in enumerate((src_ref, dst_ref, live_ref)):
        for h in range(2):
            info[0, 2 * row + h : 2 * row + h + 1, :] = ref[h * 128 : (h + 1) * 128].reshape(1, 128)
    info[0, 6:8, :] = jnp.zeros((2, 128), jnp.int32)
    loads[0].wait()
    start = jnp.concatenate(
        [jnp.concatenate([sv[:, v, :], jnp.zeros((PAD - orb, 128), F32)], 0) for v in range(nv)], 0
    )
    v_own[...] = start.astype(BF16)

    def tell_other_core():
        pl.semaphore_signal(ready_sem, inc=1, device_id=sibling, device_id_type=MESH)

    @pl.when(c == 0)
    def _():
        @pl.when(at_end)
        def _():
            pl.semaphore_wait(barrier, 9)

        @pl.when(jnp.logical_not(at_end))
        def _():
            pl.semaphore_wait(barrier, 8)

        tell_other_core()

    @pl.when(c == 1)
    def _():
        pl.semaphore_wait(ready_sem, 1)

    sent = []

    def copy_to(i, a, b, dev, own=None):
        return pltpu.make_async_remote_copy(
            src_ref=a, dst_ref=b, send_sem=send_sem.at[i if own is None else own], recv_sem=recv_sem.at[i],
            device_id=dev, device_id_type=MESH,
        )

    def send(i, a, b, dev):
        cp = copy_to(i, a, b, dev)
        cp.start()
        sent.append(cp)
        return cp

    info_in = [send(k, info.at[0], info.at[k], same[k]) for k in (1, 2, 3)]
    feat_near = copy_to(0, feat, ghost, (before, z * 2 + 1))
    feat_far = copy_to(17, feat, via, (flip_before, z * 2 + 1))
    feat_via = copy_to(0, via, ghost, (flip, (3 - z) * 2 + 1), 18)
    pass_on = copy_to(9, ghost, ghost, sibling)

    @pl.when((c == 1) & at_start)
    def _():
        feat_far.start()

    @pl.when((c == 1) & jnp.logical_not(at_start))
    def _():
        feat_near.start()

    rad_in = [send(3 + k, rad.at[0], rad.at[k], same[k]) for k in (1, 3, 2)]

    @pl.when((c == 1) & at_end & (flip > d))
    def _():
        feat_far.wait_recv()
        feat_via.start()

    def make_onehot(k, r):
        s, t = 2 * k + r, 4 * r + k
        rows = lax.broadcasted_iota(jnp.int32, (256, 128), 0)
        for h in range(2):
            lanes = slice(h * 128, (h + 1) * 128)
            onehot[s, 0:128, lanes] = jnp.where(rows[:128] == info[t, h : h + 1, :], 1.0, 0.0).astype(BF16)
            to = jnp.where(rows == info[t, 2 + h : 3 + h, :], 1.0, 0.0).astype(BF16)
            onehot[s, 128:384, lanes] = to
            if r == 0:
                onehot[s, 384:512, lanes] = to[128:]

    make_onehot(0, 0)
    for cp in info_in:
        cp.wait_recv()
    info_sib = send(8, info.at[0:4], info.at[4:8], sibling)
    for cp in loads[2:7]:
        cp.wait()

    wdt[...] = transposed(wd[...])
    for layer in range(layers):
        wht[layer] = transposed(wh[layer])
    wrt[...] = transposed(wr[...])
    rows = lax.broadcasted_iota(jnp.int32, (13 * PAD, 169), 0)
    cols = lax.broadcasted_iota(jnp.int32, (13 * PAD, 169), 1)
    outer, inner = lax.shift_right_logical(rows, 4), lax.bitwise_and(rows, 15)
    spread = jnp.where((inner < orb) & (cols == outer * orb + inner), 1.0, 0.0).astype(BF16)
    wa[...] = mm(spread, wo[...]).astype(BF16)
    rows = lax.broadcasted_iota(jnp.int32, (13 * PAD, 13 * PAD), 0)
    cols = lax.broadcasted_iota(jnp.int32, (13 * PAD, 13 * PAD), 1)
    outer, inner = lax.shift_right_logical(rows, 4), lax.bitwise_and(rows, 15)
    pb[...] = jnp.where((inner < orb) & (cols == inner * PAD + outer), 1.0, 0.0).astype(BF16)

    def halves(x):
        top = x.astype(BF16)
        return top, (x - top.astype(F32)).astype(BF16)

    for n, w in enumerate((transposed(ws[...]), wdt[...])):
        proj[0, :, n * 128 : (n + 1) * 128], proj[1, :, n * 128 : (n + 1) * 128] = halves(mm_nt(w, feat[...]))

    for k in range(1, CHIPS):
        make_onehot(k, 0)

    @pl.when(c == 1)
    def _():
        pl.semaphore_wait(barrier, 4)
        tell_other_core()

    @pl.when(c == 0)
    def _():
        pl.semaphore_wait(ready_sem, 1)

    vgh_in = send(7, v_own, v_gh, left)

    @pl.when((c == 1) & at_end & (flip < d))
    def _():
        feat_far.wait_recv()
        feat_via.start()

    info_sib.wait_recv()
    for k in range(CHIPS):
        make_onehot(k, 1)
    @pl.when(c == 1)
    def _():
        feat_near.wait_recv()
        pass_on.start()

    @pl.when(c == 0)
    def _():
        pass_on.wait_recv()

    proj[2, :, 0:128], proj[2, :, 128:256] = halves(mm_nt(wdt[...], ghost[...]))

    arrived = dict(zip((1, 3, 2), rad_in))
    h_in = []
    for batch in ((0, 1, 3), (2,)):
        for k in batch:
            if k:
                arrived[k].wait_recv()
        pre = [
            mm(proj[0], onehot[2 * k, 0:256, :]) + mm(proj[1], onehot[2 * k, 0:256, :]) + mm_nt(wrt[...], rad[k])
            for k in batch
        ]
        hidden = [silu(p + mm(proj[2], onehot[2 * k, 256:512, :])).astype(BF16) for p, k in zip(pre, batch)]
        for layer in range(layers):
            hidden = [(h.astype(F32) + silu(mm(wht[layer], h))).astype(BF16) for h in hidden]
        for h, k in zip(hidden, batch):
            live = jnp.concatenate([info[k, 4:5, :], info[k, 5:6, :]], 1).astype(F32)
            ha[2 * k] = (mm(wa[...], h) * live).astype(BF16)
            h_in.append(send(10 + k, ha.at[2 * k], ha.at[2 * k + 1], sibling))
            if k == 0:
                blocks_ref[...] = (mm(wo[...], h) * live).astype(BF16)

    def to_targets(s, vec, h):
        xs[s] = mm(vec, onehot[s, 0:128, :]).reshape(nv, PAD, 256)
        acc = jnp.zeros((nv, PAD, 256), F32)
        for a in range(orb):
            acc += h[s, a * PAD : (a + 1) * PAD, :].astype(F32)[None] * xs[s, :, a : a + 1, :]
        return mm_nt(acc.reshape(nv * PAD, 256).astype(BF16), onehot[s, 128:384, :])

    def to_sources(s, vec):
        xt[s] = mm(vec, onehot[s, 128:384, :]).reshape(nv, PAD, 256)
        acc = jnp.zeros((nv, PAD, 256), F32)
        for b in range(orb):
            acc += hb[s, b * PAD : (b + 1) * PAD, :][None] * xt[s, :, b : b + 1, :]
        return mm_nt(acc.reshape(nv * PAD, 256).astype(BF16), onehot[s, 0:128, :])

    own = v_own[...]
    p_t = jnp.zeros((nv * PAD, 256), F32)
    p_s = jnp.zeros((nv * PAD, 128), F32)
    for s in range(0, 2 * CHIPS, 2):
        p_t += to_targets(s, own, ha)
    for cp in h_in:
        cp.wait_recv()
    for s in range(1, 2 * CHIPS, 2):
        p_t += to_targets(s, own, ha)
    part_gh = p_t[:, 128:]
    gh_out[...] = part_gh.astype(BF16)
    gh_in_cp = send(14, gh_out, gh_in, right)
    vgh_in.wait_recv()
    both = jnp.concatenate([own, v_gh[...]], 1)
    for s in range(2 * CHIPS):
        hb[s] = mm(pb[...], ha[s])
        p_s += to_sources(s, both)
    part_own = p_s + p_t[:, :128]
    own_out[...] = part_own.astype(BF16)
    own_in_cp = send(15, own_out, own_in, left)

    for s in range(2 * CHIPS):
        hf[s] = ha[s].astype(F32)
    gh_in_cp.wait_recv()
    own1 = (part_own + gh_in[...].astype(F32)).astype(BF16)
    p_t = jnp.zeros((nv * PAD, 256), F32)
    for s in range(2 * CHIPS):
        p_t += to_targets(s, own1, hf)
    gh2_out[...] = p_t[:, 128:].astype(BF16)
    gh2_in_cp = send(16, gh2_out, gh2_in, right)
    own_in_cp.wait_recv()
    gh1 = (part_gh + own_in[...].astype(F32)).astype(BF16)
    both1 = jnp.concatenate([own1, gh1], 1)
    p_s = jnp.zeros((nv * PAD, 128), F32)
    for s in range(2 * CHIPS):
        p_s += to_sources(s, both1)
    second = 2.0 * (p_s + p_t[:, :128])
    for cp in sent:
        cp.wait_send()

    @pl.when(c == 1)
    def _():
        pass_on.wait_send()

    @pl.when((c == 1) & at_start)
    def _():
        feat_far.wait_send()

    @pl.when((c == 1) & jnp.logical_not(at_start))
    def _():
        feat_near.wait_send()

    @pl.when((c == 1) & at_end)
    def _():
        feat_via.wait_send()

    gh2_in_cp.wait_recv()
    second = second + 2.0 * gh2_in[...].astype(F32)
    for v in range(nv):
        out_ref[:, v, :] = second[v * PAD : v * PAD + orb] - sv[:, v, :]


def on_device(node_feat, radial, edge_src, edge_dst, edge_live, w_src, w_dst, w_radial, w_hidden, w_out, start_vectors):
    anywhere = pl.BlockSpec(memory_space=pltpu.HBM)
    vmem = pl.BlockSpec(memory_space=pltpu.VMEM)
    edges = radial.shape[0]
    start_vectors = jnp.transpose(start_vectors, (1, 0, 2))
    orb, nv, atoms = start_vectors.shape
    width = node_feat.shape[1]
    rows = 13 * PAD
    vec = nv * PAD

    def scratch(*shape, dtype=BF16):
        return pltpu.VMEM(shape, dtype)

    pair_blocks, filtered = pl.pallas_call(
        kernel,
        out_shape=(
            pltpu.VMEM((w_out.shape[0], edges), BF16),
            pltpu.VMEM(start_vectors.shape, F32),
        ),
        in_specs=[anywhere] * 11,
        out_specs=(vmem, vmem),
        scratch_shapes=[scratch(edges, dtype=jnp.int32)] * 3
        + [
            scratch(atoms, width),
            scratch(atoms, width),
            scratch(atoms, width),
            scratch(CHIPS, edges, radial.shape[1]),
            scratch(*w_src.shape),
            scratch(*w_dst.shape),
            scratch(*w_radial.shape),
            scratch(*w_hidden.shape),
            scratch(*w_out.shape),
            scratch(*start_vectors.shape, dtype=F32),
            scratch(8, 8, 128, dtype=jnp.int32),
            scratch(8, 4 * atoms, edges),
            scratch(8, rows, edges),
            scratch(8, rows, edges, dtype=F32),
            scratch(8, rows, edges, dtype=F32),
            scratch(8, nv, PAD, edges, dtype=F32),
            scratch(8, nv, PAD, edges, dtype=F32),
            scratch(vec, atoms),
            scratch(vec, atoms),
            scratch(3, width, 2 * atoms),
            scratch(*w_hidden.shape),
            scratch(width, radial.shape[1]),
            scratch(*w_dst.shape),
            scratch(rows, width),
            scratch(rows, rows),
        ]
        + [scratch(vec, atoms)] * 6
        + [
            pltpu.SemaphoreType.DMA((11,)),
            pltpu.SemaphoreType.DMA((19,)),
            pltpu.SemaphoreType.DMA((19,)),
            pltpu.SemaphoreType.REGULAR,
        ],
        compiler_params=pltpu.CompilerParams(
            collective_id=0, has_side_effects=True, vmem_limit_bytes=60 * 1024 * 1024
        ),
        name="pair_filter",
    )(node_feat, radial, edge_src, edge_dst, edge_live, w_src, w_dst, w_radial, w_hidden, w_out, start_vectors)
    return pair_blocks, jnp.transpose(filtered, (1, 0, 2))


def solution(mesh):
    in_specs = (
        P("space", None),
        P(("space", "vec"), None),
        P(("space", "vec")),
        P(("space", "vec")),
        P(("space", "vec")),
        P(),
        P(),
        P(),
        P(),
        P(),
        P("vec", None, "space"),
    )
    out_specs = (P(None, ("space", "vec")), P("vec", None, "space"))
    return jax.shard_map(
        on_device, mesh=mesh, in_specs=in_specs, out_specs=out_specs, check_vma=False
    )
```

```python
import math

import jax
import jax.numpy as jnp
from jax import lax
from jax.experimental import pallas as pl
from jax.experimental.pallas import tpu as pltpu
from jax.sharding import PartitionSpec as P

F32, BF16 = jnp.float32, jnp.bfloat16
MESH = pl.DeviceIdType.MESH
CHIPS = 4
PAD = 16


def silu(v):
    half = 0.5 * v
    return half + half * jnp.tanh(half)


def mm(a, b):
    return jnp.dot(a, b, preferred_element_type=F32)


def mm_nt(a, b):
    return lax.dot_general(a, b, (((1,), (1,)), ((), ())), preferred_element_type=F32)


def transposed(x):
    return x.astype(F32).T.astype(BF16)


def kernel(
    feat_hbm, radial_hbm, src_hbm, dst_hbm, live_hbm, ws_hbm, wd_hbm, wr_hbm, wh_hbm, wo_hbm, sv_hbm,
    blocks_ref, out_ref,
    src_ref, dst_ref, live_ref,
    feat, ghost, via, rad, ws, wd, wr, wh, wo, sv,
    info, onehot, ha, hf, hb, xs, xt,
    v_own, v_gh, proj, wht, wrt, wdt, wa, pb,
    gh_out, own_out, gh_in, own_in, gh2_out, gh2_in,
    local_sem, send_sem, recv_sem, ready_sem,
):
    n_space = lax.axis_size("space")
    d = lax.axis_index("space")
    j = lax.axis_index("vec")
    z, c = j // 2, j % 2
    zk = [z, z + 1 - 2 * (z % 2), (z + 2) % 4, 3 - z]
    before, after = lax.rem(d + n_space - 1, n_space), lax.rem(d + 1, n_space)
    left, right = (before, j), (after, j)
    same = [(d, zk[k] * 2 + c) for k in range(CHIPS)]
    sibling = (d, z * 2 + 1 - c)
    at_end, at_start = d % 4 == 3, d % 4 == 0
    flip = d + 4 - 8 * (d // 4 % 2)
    flip_before = before + 4 - 8 * (before // 4 % 2)
    flip_after = lax.rem(flip + 1, n_space)
    orb, nv = out_ref.shape[:2]
    layers = wh.shape[0]

    barrier = pltpu.get_barrier_semaphore()

    def hello(dev):
        pl.semaphore_signal(barrier, inc=1, device_id=dev, device_id_type=MESH)

    @pl.when((c == 1) & at_end)
    def _():
        hello((flip, (3 - z) * 2 + 1))
        hello((flip_after, z * 2 + 1))

    @pl.when((c == 1) & jnp.logical_not(at_end))
    def _():
        hello((after, z * 2 + 1))

    for nb in (after, before):
        hello((nb, z * 2))
    for k in range(1, CHIPS):
        hello((d, zk[k] * 2 + 1))

    @pl.when(c == 0)
    def _():
        hello(sibling)

    loads = []
    for i, (a, b) in enumerate(
        [(sv_hbm, sv), (feat_hbm, feat), (ws_hbm, ws), (wd_hbm, wd), (wr_hbm, wr), (wh_hbm, wh), (wo_hbm, wo), (radial_hbm, rad.at[0]), (src_hbm, src_ref), (dst_hbm, dst_ref), (live_hbm, live_ref)]
    ):
        cp = pltpu.make_async_copy(a, b, local_sem.at[i])
        cp.start()
        loads.append(cp)

    for cp in loads[7:] + loads[1:2]:
        cp.wait()
    for row, ref in enumerate((src_ref, dst_ref, live_ref)):
        for h in range(2):
            info[0, 2 * row + h : 2 * row + h + 1, :] = ref[h * 128 : (h + 1) * 128].reshape(1, 128)
    info[0, 6:8, :] = jnp.zeros((2, 128), jnp.int32)
    loads[0].wait()
    start = jnp.concatenate(
        [jnp.concatenate([sv[:, v, :], jnp.zeros((PAD - orb, 128), F32)], 0) for v in range(nv)], 0
    )
    v_own[...] = start.astype(BF16)

    def tell_other_core():
        pl.semaphore_signal(ready_sem, inc=1, device_id=sibling, device_id_type=MESH)

    @pl.when(c == 1)
    def _():
        @pl.when(at_end)
        def _():
            pl.semaphore_wait(barrier, 9)

        @pl.when(jnp.logical_not(at_end))
        def _():
            pl.semaphore_wait(barrier, 8)

        tell_other_core()

    @pl.when(c == 0)
    def _():
        pl.semaphore_wait(ready_sem, 1)

    sent = []

    def copy_to(i, a, b, dev, own=None):
        return pltpu.make_async_remote_copy(
            src_ref=a, dst_ref=b, send_sem=send_sem.at[i if own is None else own], recv_sem=recv_sem.at[i],
            device_id=dev, device_id_type=MESH,
        )

    def send(i, a, b, dev):
        cp = copy_to(i, a, b, dev)
        cp.start()
        sent.append(cp)
        return cp

    info_in = [send(k, info.at[0], info.at[k], same[k]) for k in (1, 2, 3)]
    feat_near = copy_to(0, feat, ghost, (before, z * 2 + 1))
    feat_far = copy_to(17, feat, via, (flip_before, z * 2 + 1))
    feat_via = copy_to(0, via, ghost, (flip, (3 - z) * 2 + 1), 18)
    pass_on = copy_to(9, ghost, ghost, sibling)

    @pl.when((c == 1) & at_start)
    def _():
        feat_far.start()

    @pl.when((c == 1) & jnp.logical_not(at_start))
    def _():
        feat_near.start()

    rad_in = [send(3 + k, rad.at[0], rad.at[k], same[k]) for k in (1, 3, 2)]

    @pl.when((c == 1) & at_end & (flip > d))
    def _():
        feat_far.wait_recv()
        feat_via.start()

    def make_onehot(k, r):
        s, t = 2 * k + r, 4 * r + k
        rows = lax.broadcasted_iota(jnp.int32, (256, 128), 0)
        for h in range(2):
            lanes = slice(h * 128, (h + 1) * 128)
            onehot[s, 0:128, lanes] = jnp.where(rows[:128] == info[t, h : h + 1, :], 1.0, 0.0).astype(BF16)
            to = jnp.where(rows == info[t, 2 + h : 3 + h, :], 1.0, 0.0).astype(BF16)
            onehot[s, 128:384, lanes] = to
            if r == 0:
                onehot[s, 384:512, lanes] = to[128:]

    make_onehot(0, 0)
    for cp in info_in:
        cp.wait_recv()
    info_sib = send(8, info.at[0:4], info.at[4:8], sibling)
    for cp in loads[2:7]:
        cp.wait()

    wdt[...] = transposed(wd[...])
    for layer in range(layers):
        wht[layer] = transposed(wh[layer])
    wrt[...] = transposed(wr[...])
    rows = lax.broadcasted_iota(jnp.int32, (13 * PAD, 169), 0)
    cols = lax.broadcasted_iota(jnp.int32, (13 * PAD, 169), 1)
    outer, inner = lax.shift_right_logical(rows, 4), lax.bitwise_and(rows, 15)
    spread = jnp.where((inner < orb) & (cols == outer * orb + inner), 1.0, 0.0).astype(BF16)
    wa[...] = mm(spread, wo[...]).astype(BF16)
    rows = lax.broadcasted_iota(jnp.int32, (13 * PAD, 13 * PAD), 0)
    cols = lax.broadcasted_iota(jnp.int32, (13 * PAD, 13 * PAD), 1)
    outer, inner = lax.shift_right_logical(rows, 4), lax.bitwise_and(rows, 15)
    pb[...] = jnp.where((inner < orb) & (cols == inner * PAD + outer), 1.0, 0.0).astype(BF16)

    def halves(x):
        top = x.astype(BF16)
        return top, (x - top.astype(F32)).astype(BF16)

    for n, w in enumerate((transposed(ws[...]), wdt[...])):
        proj[0, :, n * 128 : (n + 1) * 128], proj[1, :, n * 128 : (n + 1) * 128] = halves(mm_nt(w, feat[...]))

    for k in range(1, CHIPS):
        make_onehot(k, 0)

    @pl.when(c == 0)
    def _():
        pl.semaphore_wait(barrier, 4)
        tell_other_core()

    @pl.when(c == 1)
    def _():
        pl.semaphore_wait(ready_sem, 1)

    vgh_in = send(7, v_own, v_gh, left)

    @pl.when((c == 1) & at_end & (flip < d))
    def _():
        feat_far.wait_recv()
        feat_via.start()

    info_sib.wait_recv()
    for k in range(CHIPS):
        make_onehot(k, 1)
    @pl.when(c == 1)
    def _():
        feat_near.wait_recv()
        pass_on.start()

    @pl.when(c == 0)
    def _():
        pass_on.wait_recv()

    proj[2, :, 0:128], proj[2, :, 128:256] = halves(mm_nt(wdt[...], ghost[...]))

    arrived = dict(zip((1, 3, 2), rad_in))
    h_in = {}
    for batch in ((0, 1, 3), (2,)):
        for k in batch:
            if k:
                arrived[k].wait_recv()
        pre = [
            mm(proj[0], onehot[2 * k, 0:256, :]) + mm(proj[1], onehot[2 * k, 0:256, :]) + mm_nt(wrt[...], rad[k])
            for k in batch
        ]
        hidden = [silu(p + mm(proj[2], onehot[2 * k, 256:512, :])).astype(BF16) for p, k in zip(pre, batch)]
        for layer in range(layers):
            hidden = [(h.astype(F32) + silu(mm(wht[layer], h))).astype(BF16) for h in hidden]
        for h, k in zip(hidden, batch):
            live = jnp.concatenate([info[k, 4:5, :], info[k, 5:6, :]], 1).astype(F32)
            ha[2 * k] = (mm(wa[...], h) * live).astype(BF16)
            h_in[k] = send(10 + k, ha.at[2 * k], ha.at[2 * k + 1], sibling)
            if k == 0:
                blocks_ref[...] = (mm(wo[...], h) * live).astype(BF16)

    def to_targets(s, vec, h):
        xs[s] = mm(vec, onehot[s, 0:128, :]).reshape(nv, PAD, 256)
        acc = jnp.zeros((nv, PAD, 256), F32)
        for a in range(orb):
            acc += h[s, a * PAD : (a + 1) * PAD, :].astype(F32)[None] * xs[s, :, a : a + 1, :]
        return mm_nt(acc.reshape(nv * PAD, 256).astype(BF16), onehot[s, 128:384, :])

    def to_sources(s, vec):
        xt[s] = mm(vec, onehot[s, 128:384, :]).reshape(nv, PAD, 256)
        acc = jnp.zeros((nv, PAD, 256), F32)
        for b in range(orb):
            acc += hb[s, b * PAD : (b + 1) * PAD, :][None] * xt[s, :, b : b + 1, :]
        return mm_nt(acc.reshape(nv * PAD, 256).astype(BF16), onehot[s, 0:128, :])

    own = v_own[...]
    p_t = jnp.zeros((nv * PAD, 256), F32)
    p_s = jnp.zeros((nv * PAD, 128), F32)
    for k in range(CHIPS):
        p_t += to_targets(2 * k, own, ha)
    for k in (0, 1, 3):
        h_in[k].wait_recv()
    for k in (0, 1, 3):
        p_t += to_targets(2 * k + 1, own, ha)
    h_in[2].wait_recv()
    p_t += to_targets(5, own, ha)
    part_gh = p_t[:, 128:]
    gh_out[...] = part_gh.astype(BF16)
    gh_in_cp = send(14, gh_out, gh_in, right)
    vgh_in.wait_recv()
    both = jnp.concatenate([own, v_gh[...]], 1)
    for s in range(2 * CHIPS):
        hb[s] = mm(pb[...], ha[s])
        p_s += to_sources(s, both)
    part_own = p_s + p_t[:, :128]
    own_out[...] = part_own.astype(BF16)
    own_in_cp = send(15, own_out, own_in, left)

    for s in range(2 * CHIPS):
        hf[s] = ha[s].astype(F32)
    gh_in_cp.wait_recv()
    own1 = (part_own + gh_in[...].astype(F32)).astype(BF16)
    p_t = jnp.zeros((nv * PAD, 256), F32)
    for s in range(2 * CHIPS):
        p_t += to_targets(s, own1, hf)
    gh2_out[...] = p_t[:, 128:].astype(BF16)
    gh2_in_cp = send(16, gh2_out, gh2_in, right)
    own_in_cp.wait_recv()
    gh1 = (part_gh + own_in[...].astype(F32)).astype(BF16)
    both1 = jnp.concatenate([own1, gh1], 1)
    p_s = jnp.zeros((nv * PAD, 128), F32)
    for s in range(2 * CHIPS):
        p_s += to_sources(s, both1)
    second = 2.0 * (p_s + p_t[:, :128])
    for cp in sent:
        cp.wait_send()

    @pl.when(c == 1)
    def _():
        pass_on.wait_send()

    @pl.when((c == 1) & at_start)
    def _():
        feat_far.wait_send()

    @pl.when((c == 1) & jnp.logical_not(at_start))
    def _():
        feat_near.wait_send()

    @pl.when((c == 1) & at_end)
    def _():
        feat_via.wait_send()

    gh2_in_cp.wait_recv()
    second = second + 2.0 * gh2_in[...].astype(F32)
    for v in range(nv):
        out_ref[:, v, :] = second[v * PAD : v * PAD + orb] - sv[:, v, :]


def on_device(node_feat, radial, edge_src, edge_dst, edge_live, w_src, w_dst, w_radial, w_hidden, w_out, start_vectors):
    anywhere = pl.BlockSpec(memory_space=pltpu.HBM)
    vmem = pl.BlockSpec(memory_space=pltpu.VMEM)
    edges = radial.shape[0]
    start_vectors = jnp.transpose(start_vectors, (1, 0, 2))
    orb, nv, atoms = start_vectors.shape
    width = node_feat.shape[1]
    rows = 13 * PAD
    vec = nv * PAD

    def scratch(*shape, dtype=BF16):
        return pltpu.VMEM(shape, dtype)

    pair_blocks, filtered = pl.pallas_call(
        kernel,
        out_shape=(
            pltpu.VMEM((w_out.shape[0], edges), BF16),
            pltpu.VMEM(start_vectors.shape, F32),
        ),
        in_specs=[anywhere] * 11,
        out_specs=(vmem, vmem),
        scratch_shapes=[scratch(edges, dtype=jnp.int32)] * 3
        + [
            scratch(atoms, width),
            scratch(atoms, width),
            scratch(atoms, width),
            scratch(CHIPS, edges, radial.shape[1]),
            scratch(*w_src.shape),
            scratch(*w_dst.shape),
            scratch(*w_radial.shape),
            scratch(*w_hidden.shape),
            scratch(*w_out.shape),
            scratch(*start_vectors.shape, dtype=F32),
            scratch(8, 8, 128, dtype=jnp.int32),
            scratch(8, 4 * atoms, edges),
            scratch(8, rows, edges),
            scratch(8, rows, edges, dtype=F32),
            scratch(8, rows, edges, dtype=F32),
            scratch(8, nv, PAD, edges, dtype=F32),
            scratch(8, nv, PAD, edges, dtype=F32),
            scratch(vec, atoms),
            scratch(vec, atoms),
            scratch(3, width, 2 * atoms),
            scratch(*w_hidden.shape),
            scratch(width, radial.shape[1]),
            scratch(*w_dst.shape),
            scratch(rows, width),
            scratch(rows, rows),
        ]
        + [scratch(vec, atoms)] * 6
        + [
            pltpu.SemaphoreType.DMA((11,)),
            pltpu.SemaphoreType.DMA((19,)),
            pltpu.SemaphoreType.DMA((19,)),
            pltpu.SemaphoreType.REGULAR,
        ],
        compiler_params=pltpu.CompilerParams(
            collective_id=0, has_side_effects=True, vmem_limit_bytes=60 * 1024 * 1024
        ),
        name="pair_filter",
    )(node_feat, radial, edge_src, edge_dst, edge_live, w_src, w_dst, w_radial, w_hidden, w_out, start_vectors)
    return pair_blocks, jnp.transpose(filtered, (1, 0, 2))


def solution(mesh):
    in_specs = (
        P("space", None),
        P(("space", "vec"), None),
        P(("space", "vec")),
        P(("space", "vec")),
        P(("space", "vec")),
        P(),
        P(),
        P(),
        P(),
        P(),
        P("vec", None, "space"),
    )
    out_specs = (P(None, ("space", "vec")), P("vec", None, "space"))
    return jax.shard_map(
        on_device, mesh=mesh, in_specs=in_specs, out_specs=out_specs, check_vma=False
    )
```

```python
import math

import jax
import jax.numpy as jnp
from jax import lax
from jax.experimental import pallas as pl
from jax.experimental.pallas import tpu as pltpu
from jax.sharding import PartitionSpec as P

F32, BF16 = jnp.float32, jnp.bfloat16
MESH = pl.DeviceIdType.MESH
CHIPS = 4
PAD = 16


def silu(v):
    half = 0.5 * v
    return half + half * jnp.tanh(half)


def mm(a, b):
    return jnp.dot(a, b, preferred_element_type=F32)


def mm_nt(a, b):
    return lax.dot_general(a, b, (((1,), (1,)), ((), ())), preferred_element_type=F32)


def transposed(x):
    return x.astype(F32).T.astype(BF16)


def kernel(
    feat_hbm, radial_hbm, src_hbm, dst_hbm, live_hbm, ws_hbm, wd_hbm, wr_hbm, wh_hbm, wo_hbm, sv_hbm,
    blocks_ref, out_ref,
    src_ref, dst_ref, live_ref,
    feat, ghost, via, rad, ws, wd, wr, wh, wo, sv,
    info, onehot, ha, hf, hb, xs, xt, ys,
    v_own, v_gh, proj, wht, wrt, wdt, wa, pb,
    gh_out, own_out, gh_in, own_in, gh2_out, gh2_in,
    local_sem, send_sem, recv_sem, ready_sem,
):
    n_space = lax.axis_size("space")
    d = lax.axis_index("space")
    j = lax.axis_index("vec")
    z, c = j // 2, j % 2
    zk = [z, z + 1 - 2 * (z % 2), (z + 2) % 4, 3 - z]
    before, after = lax.rem(d + n_space - 1, n_space), lax.rem(d + 1, n_space)
    left, right = (before, j), (after, j)
    same = [(d, zk[k] * 2 + c) for k in range(CHIPS)]
    sibling = (d, z * 2 + 1 - c)
    at_end, at_start = d % 4 == 3, d % 4 == 0
    flip = d + 4 - 8 * (d // 4 % 2)
    flip_before = before + 4 - 8 * (before // 4 % 2)
    flip_after = lax.rem(flip + 1, n_space)
    orb, nv = out_ref.shape[:2]
    layers = wh.shape[0]

    barrier = pltpu.get_barrier_semaphore()

    def hello(dev):
        pl.semaphore_signal(barrier, inc=1, device_id=dev, device_id_type=MESH)

    @pl.when((c == 1) & at_end)
    def _():
        hello((flip, (3 - z) * 2 + 1))
        hello((flip_after, z * 2 + 1))

    @pl.when((c == 1) & jnp.logical_not(at_end))
    def _():
        hello((after, z * 2 + 1))

    for nb in (after, before):
        hello((nb, z * 2))
    for k in range(1, CHIPS):
        hello((d, zk[k] * 2 + 1))

    @pl.when(c == 0)
    def _():
        hello(sibling)

    loads = []
    for i, (a, b) in enumerate(
        [(sv_hbm, sv), (feat_hbm, feat), (ws_hbm, ws), (wd_hbm, wd), (wr_hbm, wr), (wh_hbm, wh), (wo_hbm, wo), (radial_hbm, rad.at[0]), (src_hbm, src_ref), (dst_hbm, dst_ref), (live_hbm, live_ref)]
    ):
        cp = pltpu.make_async_copy(a, b, local_sem.at[i])
        cp.start()
        loads.append(cp)

    for cp in loads[7:] + loads[1:2]:
        cp.wait()
    for row, ref in enumerate((src_ref, dst_ref, live_ref)):
        for h in range(2):
            info[0, 2 * row + h : 2 * row + h + 1, :] = ref[h * 128 : (h + 1) * 128].reshape(1, 128)
    info[0, 6:8, :] = jnp.zeros((2, 128), jnp.int32)
    loads[0].wait()
    start = jnp.concatenate(
        [jnp.concatenate([sv[:, v, :], jnp.zeros((PAD - orb, 128), F32)], 0) for v in range(nv)], 0
    )
    v_own[...] = start.astype(BF16)

    def tell_other_core():
        pl.semaphore_signal(ready_sem, inc=1, device_id=sibling, device_id_type=MESH)

    @pl.when(c == 1)
    def _():
        @pl.when(at_end)
        def _():
            pl.semaphore_wait(barrier, 9)

        @pl.when(jnp.logical_not(at_end))
        def _():
            pl.semaphore_wait(barrier, 8)

        tell_other_core()

    @pl.when(c == 0)
    def _():
        pl.semaphore_wait(ready_sem, 1)

    sent = []

    def copy_to(i, a, b, dev, own=None):
        return pltpu.make_async_remote_copy(
            src_ref=a, dst_ref=b, send_sem=send_sem.at[i if own is None else own], recv_sem=recv_sem.at[i],
            device_id=dev, device_id_type=MESH,
        )

    def send(i, a, b, dev):
        cp = copy_to(i, a, b, dev)
        cp.start()
        sent.append(cp)
        return cp

    info_in = [send(k, info.at[0], info.at[k], same[k]) for k in (1, 2, 3)]
    feat_near = copy_to(0, feat, ghost, (before, z * 2 + 1))
    feat_far = copy_to(17, feat, via, (flip_before, z * 2 + 1))
    feat_via = copy_to(0, via, ghost, (flip, (3 - z) * 2 + 1), 18)
    pass_on = copy_to(9, ghost, ghost, sibling)

    @pl.when((c == 1) & at_start)
    def _():
        feat_far.start()

    @pl.when((c == 1) & jnp.logical_not(at_start))
    def _():
        feat_near.start()

    rad_in = [send(3 + k, rad.at[0], rad.at[k], same[k]) for k in (1, 3, 2)]

    @pl.when((c == 1) & at_end & (flip > d))
    def _():
        feat_far.wait_recv()
        feat_via.start()

    def make_onehot(k, r):
        s, t = 2 * k + r, 4 * r + k
        rows = lax.broadcasted_iota(jnp.int32, (256, 128), 0)
        for h in range(2):
            lanes = slice(h * 128, (h + 1) * 128)
            onehot[s, 0:128, lanes] = jnp.where(rows[:128] == info[t, h : h + 1, :], 1.0, 0.0).astype(BF16)
            to = jnp.where(rows == info[t, 2 + h : 3 + h, :], 1.0, 0.0).astype(BF16)
            onehot[s, 128:384, lanes] = to
            if r == 0:
                onehot[s, 384:512, lanes] = to[128:]

    make_onehot(0, 0)
    for cp in info_in:
        cp.wait_recv()
    info_sib = send(8, info.at[0:4], info.at[4:8], sibling)
    for cp in loads[2:7]:
        cp.wait()

    wdt[...] = transposed(wd[...])
    for layer in range(layers):
        wht[layer] = transposed(wh[layer])
    wrt[...] = transposed(wr[...])
    rows = lax.broadcasted_iota(jnp.int32, (13 * PAD, 169), 0)
    cols = lax.broadcasted_iota(jnp.int32, (13 * PAD, 169), 1)
    outer, inner = lax.shift_right_logical(rows, 4), lax.bitwise_and(rows, 15)
    spread = jnp.where((inner < orb) & (cols == outer * orb + inner), 1.0, 0.0).astype(BF16)
    wa[...] = mm(spread, wo[...]).astype(BF16)
    rows = lax.broadcasted_iota(jnp.int32, (13 * PAD, 13 * PAD), 0)
    cols = lax.broadcasted_iota(jnp.int32, (13 * PAD, 13 * PAD), 1)
    outer, inner = lax.shift_right_logical(rows, 4), lax.bitwise_and(rows, 15)
    pb[...] = jnp.where((inner < orb) & (cols == inner * PAD + outer), 1.0, 0.0).astype(BF16)

    def halves(x):
        top = x.astype(BF16)
        return top, (x - top.astype(F32)).astype(BF16)

    for n, w in enumerate((transposed(ws[...]), wdt[...])):
        proj[0, :, n * 128 : (n + 1) * 128], proj[1, :, n * 128 : (n + 1) * 128] = halves(mm_nt(w, feat[...]))

    for k in range(1, CHIPS):
        make_onehot(k, 0)

    @pl.when(c == 0)
    def _():
        pl.semaphore_wait(barrier, 4)
        tell_other_core()

    @pl.when(c == 1)
    def _():
        pl.semaphore_wait(ready_sem, 1)

    vgh_in = send(7, v_own, v_gh, left)

    @pl.when((c == 1) & at_end & (flip < d))
    def _():
        feat_far.wait_recv()
        feat_via.start()

    info_sib.wait_recv()
    for k in range(CHIPS):
        make_onehot(k, 1)
    @pl.when(c == 1)
    def _():
        feat_near.wait_recv()
        pass_on.start()

    @pl.when(c == 0)
    def _():
        pass_on.wait_recv()

    proj[2, :, 0:128], proj[2, :, 128:256] = halves(mm_nt(wdt[...], ghost[...]))

    arrived = dict(zip((1, 3, 2), rad_in))
    h_in = {}
    for batch in ((0, 1, 3), (2,)):
        for k in batch:
            if k:
                arrived[k].wait_recv()
        pre = [
            mm(proj[0], onehot[2 * k, 0:256, :]) + mm(proj[1], onehot[2 * k, 0:256, :]) + mm_nt(wrt[...], rad[k])
            for k in batch
        ]
        hidden = [silu(p + mm(proj[2], onehot[2 * k, 256:512, :])).astype(BF16) for p, k in zip(pre, batch)]
        for layer in range(layers):
            hidden = [(h.astype(F32) + silu(mm(wht[layer], h))).astype(BF16) for h in hidden]
        for h, k in zip(hidden, batch):
            live = jnp.concatenate([info[k, 4:5, :], info[k, 5:6, :]], 1).astype(F32)
            ha[2 * k] = (mm(wa[...], h) * live).astype(BF16)
            h_in[k] = send(10 + k, ha.at[2 * k], ha.at[2 * k + 1], sibling)
            if k == 0:
                blocks_ref[...] = (mm(wo[...], h) * live).astype(BF16)

    def target_products(s, vec, h):
        xs[s] = mm(vec, onehot[s, 0:128, :]).reshape(nv, PAD, 256)
        acc = jnp.zeros((nv, PAD, 256), F32)
        for a in range(orb):
            acc += h[s, a * PAD : (a + 1) * PAD, :].astype(F32)[None] * xs[s, :, a : a + 1, :]
        return acc.reshape(nv * PAD, 256).astype(BF16)

    def to_targets(s, vec, h):
        return mm_nt(target_products(s, vec, h), onehot[s, 128:384, :])

    def to_sources(s, vec):
        xt[s] = mm(vec, onehot[s, 128:384, :]).reshape(nv, PAD, 256)
        acc = jnp.zeros((nv, PAD, 256), F32)
        for b in range(orb):
            acc += hb[s, b * PAD : (b + 1) * PAD, :][None] * xt[s, :, b : b + 1, :]
        return mm_nt(acc.reshape(nv * PAD, 256).astype(BF16), onehot[s, 0:128, :])

    own = v_own[...]
    p_t = jnp.zeros((nv * PAD, 256), F32)
    p_s = jnp.zeros((nv * PAD, 128), F32)
    for k in range(CHIPS):
        p_t += to_targets(2 * k, own, ha)
    for k in (0, 1, 3):
        h_in[k].wait_recv()
    for k in (0, 1, 3):
        p_t += to_targets(2 * k + 1, own, ha)
    h_in[2].wait_recv()
    p_t += to_targets(5, own, ha)
    part_gh = p_t[:, 128:]
    gh_out[...] = part_gh.astype(BF16)
    gh_in_cp = send(14, gh_out, gh_in, right)
    vgh_in.wait_recv()
    both = jnp.concatenate([own, v_gh[...]], 1)
    for s in range(2 * CHIPS):
        hb[s] = mm(pb[...], ha[s])
        p_s += to_sources(s, both)
    part_own = p_s + p_t[:, :128]
    own_out[...] = part_own.astype(BF16)
    own_in_cp = send(15, own_out, own_in, left)

    for s in range(2 * CHIPS):
        hf[s] = ha[s].astype(F32)
    gh_in_cp.wait_recv()
    own1 = (part_own + gh_in[...].astype(F32)).astype(BF16)
    p_g = jnp.zeros((nv * PAD, 128), F32)
    for s in range(2 * CHIPS):
        ys[s] = target_products(s, own1, hf)
        p_g += mm_nt(ys[s], onehot[s, 256:384, :])
    gh2_out[...] = p_g.astype(BF16)
    gh2_in_cp = send(16, gh2_out, gh2_in, right)
    own_in_cp.wait_recv()
    gh1 = (part_gh + own_in[...].astype(F32)).astype(BF16)
    both1 = jnp.concatenate([own1, gh1], 1)
    p_s = jnp.zeros((nv * PAD, 128), F32)
    for s in range(2 * CHIPS):
        p_s += mm_nt(ys[s], onehot[s, 128:256, :]) + to_sources(s, both1)
    second = 2.0 * p_s
    for cp in sent:
        cp.wait_send()

    @pl.when(c == 1)
    def _():
        pass_on.wait_send()

    @pl.when((c == 1) & at_start)
    def _():
        feat_far.wait_send()

    @pl.when((c == 1) & jnp.logical_not(at_start))
    def _():
        feat_near.wait_send()

    @pl.when((c == 1) & at_end)
    def _():
        feat_via.wait_send()

    gh2_in_cp.wait_recv()
    second = second + 2.0 * gh2_in[...].astype(F32)
    for v in range(nv):
        out_ref[:, v, :] = second[v * PAD : v * PAD + orb] - sv[:, v, :]


def on_device(node_feat, radial, edge_src, edge_dst, edge_live, w_src, w_dst, w_radial, w_hidden, w_out, start_vectors):
    anywhere = pl.BlockSpec(memory_space=pltpu.HBM)
    vmem = pl.BlockSpec(memory_space=pltpu.VMEM)
    edges = radial.shape[0]
    start_vectors = jnp.transpose(start_vectors, (1, 0, 2))
    orb, nv, atoms = start_vectors.shape
    width = node_feat.shape[1]
    rows = 13 * PAD
    vec = nv * PAD

    def scratch(*shape, dtype=BF16):
        return pltpu.VMEM(shape, dtype)

    pair_blocks, filtered = pl.pallas_call(
        kernel,
        out_shape=(
            pltpu.VMEM((w_out.shape[0], edges), BF16),
            pltpu.VMEM(start_vectors.shape, F32),
        ),
        in_specs=[anywhere] * 11,
        out_specs=(vmem, vmem),
        scratch_shapes=[scratch(edges, dtype=jnp.int32)] * 3
        + [
            scratch(atoms, width),
            scratch(atoms, width),
            scratch(atoms, width),
            scratch(CHIPS, edges, radial.shape[1]),
            scratch(*w_src.shape),
            scratch(*w_dst.shape),
            scratch(*w_radial.shape),
            scratch(*w_hidden.shape),
            scratch(*w_out.shape),
            scratch(*start_vectors.shape, dtype=F32),
            scratch(8, 8, 128, dtype=jnp.int32),
            scratch(8, 4 * atoms, edges),
            scratch(8, rows, edges),
            scratch(8, rows, edges, dtype=F32),
            scratch(8, rows, edges, dtype=F32),
            scratch(8, nv, PAD, edges, dtype=F32),
            scratch(8, nv, PAD, edges, dtype=F32),
            scratch(8, vec, edges),
            scratch(vec, atoms),
            scratch(vec, atoms),
            scratch(3, width, 2 * atoms),
            scratch(*w_hidden.shape),
            scratch(width, radial.shape[1]),
            scratch(*w_dst.shape),
            scratch(rows, width),
            scratch(rows, rows),
        ]
        + [scratch(vec, atoms)] * 6
        + [
            pltpu.SemaphoreType.DMA((11,)),
            pltpu.SemaphoreType.DMA((19,)),
            pltpu.SemaphoreType.DMA((19,)),
            pltpu.SemaphoreType.REGULAR,
        ],
        compiler_params=pltpu.CompilerParams(
            collective_id=0, has_side_effects=True, vmem_limit_bytes=60 * 1024 * 1024
        ),
        name="pair_filter",
    )(node_feat, radial, edge_src, edge_dst, edge_live, w_src, w_dst, w_radial, w_hidden, w_out, start_vectors)
    return pair_blocks, jnp.transpose(filtered, (1, 0, 2))


def solution(mesh):
    in_specs = (
        P("space", None),
        P(("space", "vec"), None),
        P(("space", "vec")),
        P(("space", "vec")),
        P(("space", "vec")),
        P(),
        P(),
        P(),
        P(),
        P(),
        P("vec", None, "space"),
    )
    out_specs = (P(None, ("space", "vec")), P("vec", None, "space"))
    return jax.shard_map(
        on_device, mesh=mesh, in_specs=in_specs, out_specs=out_specs, check_vma=False
    )
```
